512 devices in a mesh: tiles: 128 (over y, z, core), rep: 4 (over x).
Axes of the slice: x: 4, y: 8, z: 8, core: 2. Of those that a mesh axis runs over, the one named last changes fastest.
Arguments:
- lam_tiles: bfloat16 [2048, 128, 128], P('tiles'), may hold values from -6 to 6
- int_tiles: bfloat16 [2048, 128, 128], P('tiles'), may hold values from -0.0625 to 0.0625
- task_list: int32 [65536, 4], P(('tiles', 'rep')), may hold values from 0 to 2047, as said below
- live_count: int32 [512], P(('tiles', 'rep')), may hold values from 16 to 128, as said below
- tile_mask: int32 [2048], P('tiles'), may hold values 0 or 1
- owner_map: int32 [512], replicated, may hold values from 0 to 511, as said below
Outputs:
- residual: bfloat16 [512, 128, 128], P(('tiles', 'rep'))
The draws below stay inside these ranges and needn't reach their ends.
Inputs may be any that keep to these rules, and one draw needn't show every extreme that they name: `task_list`: each row is (Lambda tile id, integral tile id, residual tile id, code 0 or 1). The Lambda tiles named by a device lie among the 16 tiles of its index of tiles. The four columns hold ids below 2048, 2048, 512 and 2. Among all slots of the devices that share an index of tiles, the integral tiles named from one owner (id // 16) are one and the same tile, and so are the residual tiles whose position lies in one owner's range (owner_map // 4); every device names every owner of both kinds in its first 128 slots. `live_count`: one device of each index of tiles uses all 128 slots. `owner_map`: A permutation of 0 to 511.
All inputs are finite; a program needn't handle non-finite values. No bound on the sum of `tile_mask` on one device may be relied on, other than what follows from the above.
Results may differ from the reference program's by a relative error of at most 0.001.
Values may be sent and summed in bfloat16 or wider, within the bound.
No kernel may reach another device: no remote copies, remote signals or barrier semaphores. Data moves between devices by JAX's collectives and lax.ppermute only.
A program may use at most 128 MiB of HBM per device.

```python
import jax
import jax.numpy as jnp
from jax import lax

TILE = 128
NL_DEV = 16
NW_DEV = 16
TASK_DEV = 128
NL = 2048
NW = 2048
RES_T = 4
NOUT = 512
N_TILES = 128
N_REP = 4
DEVICES = 512


def shared_map(key):
    return jax.random.permutation(jax.random.fold_in(key, 11), NOUT).astype(jnp.int32)


def draw_owner_map(key, part):
    return shared_map(key)


def draw_live_count(key, part):
    key = jax.random.fold_in(key, 5)
    key_full, key_rest = jax.random.split(key)
    full_rank = jax.random.randint(key_full, (N_TILES,), 0, N_REP)
    others = jax.random.randint(key_rest, (N_TILES, N_REP), max(TASK_DEV // 8, 1), TASK_DEV + 1)
    ranks = jnp.arange(N_REP)[None, :]
    return jnp.where(ranks == full_rank[:, None], TASK_DEV, others).reshape(-1).astype(jnp.int32)


def draw_task_list(key, part):
    placed = shared_map(key)
    inverse = jnp.argsort(placed).astype(jnp.int32)
    key = jax.random.fold_in(key, 3)
    keys = jax.random.split(key, 8)
    w_choice = jax.random.randint(keys[0], (N_TILES, N_TILES), 0, NW_DEV)
    o_choice = jax.random.randint(keys[1], (N_TILES, N_TILES), 0, RES_T)
    slots = jnp.arange(TASK_DEV)

    def owners(key_head, key_rest):
        scores = jax.random.randint(key_head, (DEVICES, N_TILES), 0, 2 ** 20) * N_TILES + jnp.arange(N_TILES)[None, :]
        covered = jnp.argsort(scores, axis=1).astype(jnp.int32)
        rest = jax.random.randint(key_rest, (DEVICES, TASK_DEV), 0, N_TILES)
        head = covered[:, jnp.minimum(slots, N_TILES - 1)]
        return jnp.where(slots[None, :] < N_TILES, head, rest)
    w_owner = owners(keys[2], keys[3])
    o_owner = owners(keys[4], keys[5])
    group = (jnp.arange(DEVICES) // N_REP)[:, None]
    lam_ids = group * NL_DEV + jax.random.randint(keys[6], (DEVICES, TASK_DEV), 0, NL_DEV)
    w_ids = w_owner * NW_DEV + w_choice[group, w_owner]
    o_ids = inverse[o_owner * RES_T + o_choice[group, o_owner]]
    flips = jax.random.randint(keys[7], (DEVICES, TASK_DEV), 0, 2)
    return jnp.stack([lam_ids, w_ids, o_ids, flips], axis=-1).reshape(DEVICES * TASK_DEV, 4).astype(jnp.int32)


def touch_ends(drawn, rng, low, top_value):
    index_at = [jax.random.randint(jax.random.fold_in(rng, axis), (), 0, length) for axis, length in enumerate(drawn.shape)]
    longest = drawn.shape.index(max(drawn.shape))
    neighbour = index_at[:longest] + [(index_at[longest] + 1) % drawn.shape[longest]] + index_at[longest + 1:]
    return drawn.at[tuple(index_at)].set(low).at[tuple(neighbour)].set(top_value)


def block_scale(rng, dims, shards, least, top_value):
    gain, own = 1.0, jax.random.fold_in(rng, 6)
    for position, parts in shards:
        draws = jnp.exp(jax.random.uniform(jax.random.fold_in(own, position), (parts,), jnp.float32, least / len(shards), top_value / len(shards)))
        gain = gain * jnp.repeat(draws, dims[position] // parts).reshape([-1 if axis == position else 1 for axis in range(len(dims))])
    return gain


def noise(key, extent, deviation, limit, pieces=(), held_as=jnp.bfloat16):
    gain = block_scale(key, extent, pieces, -0.22, 0.18) if pieces else 1.0
    drawn = jax.random.normal(key, extent, jnp.float32) * deviation * gain
    return jnp.minimum(jnp.maximum(drawn, -limit), limit).astype(held_as)


def setup_inputs(seed: int = 0) -> dict:
    key_of = jax.random.split(jax.random.key(seed), 7)
    return {
        "lam_tiles": noise(key_of[0], (NL, TILE, TILE), 1.0, 6.0, ((0, 128),)),
        "int_tiles": noise(key_of[1], (NW, TILE, TILE), (64 * TILE) ** -0.5, 0.0625, ((0, 128),)),
        "task_list": draw_task_list(jax.random.fold_in(key_of[6], 71), 0),
        "live_count": draw_live_count(jax.random.fold_in(key_of[6], 71), 0),
        "tile_mask": touch_ends((jax.random.randint(key_of[4], (NL,), 0, 4) < 3).astype(jnp.int32), jax.random.fold_in(key_of[4], 1), 0, 1),
        "owner_map": draw_owner_map(jax.random.fold_in(key_of[6], 71), 0),
    }


def reference(lam_tiles, int_tiles, task_list, live_count, tile_mask, owner_map):
    grouped = task_list.reshape(DEVICES, TASK_DEV, 4)
    slots = jnp.arange(TASK_DEV)

    def one_device(totals, item):
        rows, used = item
        lam_ids = rows[:, 0]
        left = lam_tiles[lam_ids].astype(jnp.float32)
        left = jnp.where(rows[:, 3][:, None, None] == 1, jnp.swapaxes(left, 1, 2), left)
        right = int_tiles[rows[:, 1]].astype(jnp.float32)
        product = jnp.einsum('tik,tkj->tij', left, right)
        keep = ((slots < used) & (tile_mask[lam_ids] == 1)).astype(jnp.float32)
        product = product * keep[:, None, None]
        places = owner_map[rows[:, 2]]
        return totals.at[places].add(product), None

    totals = jnp.zeros((NOUT, TILE, TILE), jnp.float32)
    totals, _ = lax.scan(one_device, totals, (grouped, live_count))
    return totals.astype(jnp.bfloat16)
```

```python
import jax
import jax.numpy as jnp
from jax import lax
from jax.experimental import pallas as pl
from jax.experimental.pallas import tpu as pltpu
from jax.sharding import PartitionSpec as P

VMEM = pl.BlockSpec(memory_space=pltpu.VMEM)
SMEM = pl.BlockSpec(memory_space=pltpu.SMEM)


def ring(values, steps):
    reps = lax.axis_size("rep")
    return lax.ppermute(values, "rep", [(i, (i + steps) % reps) for i in range(reps)])


def prepare_lambda(lam_ref, out_ref):
    count = lam_ref.shape[0]
    for tile in range(count):
        out_ref[tile] = lam_ref[tile].T
        out_ref[count + tile] = lam_ref[tile]
    out_ref[2 * count] = jnp.zeros_like(out_ref[2 * count])


def prepare_integrals(start_ref, int_ref, out_ref, turned):
    count, rows, _ = out_ref.shape
    start = pl.multiple_of(start_ref[0], rows)
    for tile in range(count):
        turned[tile] = int_ref[tile].T
        out_ref[tile] = turned[tile, pl.ds(start, rows), :]


def pick(asked_ref, tiles_ref, out_ref):
    def body(peer, carry):
        out_ref[peer] = tiles_ref[asked_ref[peer]]
        return carry

    lax.fori_loop(0, out_ref.shape[0], body, 0, unroll=8)


def contract(variant_ref, source_ref, lam_ref, w_ref, out_ref):
    reps = variant_ref.shape[0]

    def body(owner, carry):
        left = [w_ref[source_ref[r, owner]] for r in range(reps)]
        right = [lam_ref[variant_ref[r, owner]] for r in range(reps)]
        out_ref[owner] = jnp.dot(
            jnp.concatenate(left, axis=1),
            jnp.concatenate(right, axis=0),
            preferred_element_type=jnp.float32,
        )
        return carry

    lax.fori_loop(0, out_ref.shape[0], body, 0, unroll=4)


def add_slots(slot_ref, x_ref, out_ref):
    slots = out_ref.shape[0]

    def body(peer, sums):
        value = x_ref[peer]
        slot = slot_ref[peer]
        return tuple(s + jnp.where(slot == k, value, 0.0) for k, s in enumerate(sums))

    zero = jnp.zeros(x_ref.shape[1:], jnp.float32)
    sums = lax.fori_loop(0, x_ref.shape[0], body, (zero,) * slots, unroll=4)
    for k in range(slots):
        out_ref[k] = sums[k].astype(out_ref.dtype)


def on_device(lam_tiles, int_tiles, task_list, live_count, tile_mask, owner_map):
    tile_devs = lax.axis_size("tiles")
    reps = lax.axis_size("rep")
    tile_index = lax.axis_index("tiles")
    rep_index = lax.axis_index("rep")
    task_dev = task_list.shape[0]
    lam_dev, edge, _ = lam_tiles.shape
    int_dev = int_tiles.shape[0]
    res_tile = owner_map.shape[0] // tile_devs
    rows = edge // reps
    peers = jnp.arange(tile_devs)

    matches = task_list[:, 2:3] == jnp.arange(owner_map.shape[0])[None, :]
    places = jnp.sum(jnp.where(matches, owner_map[None, :], 0), axis=1)
    w_owner = task_list[:, 1] // int_dev
    hits_w = w_owner[:, None] == peers[None, :]
    hits_o = (places // res_tile)[:, None] == peers[None, :]
    asked = jnp.sum(jnp.where(hits_w, (task_list[:, 1] % int_dev)[:, None], 0), axis=0)
    slots = jnp.sum(jnp.where(hits_o, (places % res_tile)[:, None], 0), axis=0)
    request = asked * res_tile + slots
    request = lax.all_to_all(
        request.reshape(tile_devs, 1, 1), "tiles", split_axis=0, concat_axis=0, tiled=True
    ).reshape(-1)

    lam_local = jnp.clip(task_list[:, 0] - tile_index * lam_dev, 0, lam_dev - 1)
    mask_hits = lam_local[:, None] == jnp.arange(lam_dev)[None, :]
    kept = jnp.sum(jnp.where(mask_hits, tile_mask[None, :], 0), axis=1) == 1
    kept = kept & (jnp.arange(task_dev) < live_count[0])
    variant = jnp.where(kept, lam_local + lam_dev * task_list[:, 3], 2 * lam_dev)
    coded = variant * tile_devs + w_owner
    by_owner = jnp.sum(jnp.where(hits_o, coded[:, None], 0), axis=0)
    all_coded = jnp.stack([by_owner] + [ring(by_owner, k) for k in range(1, reps)])

    lam_all = pl.pallas_call(
        prepare_lambda,
        out_shape=jax.ShapeDtypeStruct((2 * lam_dev + 1, edge, edge), jnp.bfloat16),
        in_specs=[VMEM],
        out_specs=VMEM,
        name="prepare_lambda",
    )(lam_tiles)
    columns = pl.pallas_call(
        prepare_integrals,
        out_shape=jax.ShapeDtypeStruct((int_dev, rows, edge), jnp.bfloat16),
        in_specs=[SMEM, VMEM],
        out_specs=VMEM,
        scratch_shapes=[pltpu.VMEM((int_dev, edge, edge), jnp.bfloat16)],
        name="prepare_integrals",
    )((rep_index * rows).reshape(1), int_tiles)
    picked = pl.pallas_call(
        pick,
        out_shape=jax.ShapeDtypeStruct((tile_devs, rows, edge), jnp.bfloat16),
        in_specs=[SMEM, VMEM],
        out_specs=VMEM,
        name="pick",
    )(request // res_tile, columns)
    fetched = lax.all_to_all(picked, "tiles", split_axis=0, concat_axis=0, tiled=True)

    totals = pl.pallas_call(
        contract,
        out_shape=jax.ShapeDtypeStruct((tile_devs, rows, edge), jnp.float32),
        in_specs=[SMEM, SMEM, VMEM, VMEM],
        out_specs=VMEM,
        name="contract",
    )(all_coded // tile_devs, all_coded % tile_devs, lam_all, fetched)
    partial_tiles = lax.all_to_all(totals, "tiles", split_axis=0, concat_axis=0, tiled=True)
    summed = pl.pallas_call(
        add_slots,
        out_shape=jax.ShapeDtypeStruct((res_tile, rows, edge), jnp.bfloat16),
        in_specs=[SMEM, VMEM],
        out_specs=VMEM,
        name="add_slots",
    )(request % res_tile, partial_tiles)
    mine = lax.all_to_all(summed, "rep", split_axis=0, concat_axis=0, tiled=True)
    return mine.reshape(edge, edge).T[None]


def solution(mesh):
    placed = (
        P("tiles", None, None),
        P("tiles", None, None),
        P(("tiles", "rep"), None),
        P(("tiles", "rep")),
        P("tiles"),
        P(),
    )
    return jax.shard_map(
        on_device,
        mesh=mesh,
        in_specs=placed,
        out_specs=P(("tiles", "rep"), None, None),
        check_vma=False,
    )
```

```python
import functools

import jax
import jax.numpy as jnp
from jax import lax
from jax.experimental import pallas as pl
from jax.experimental.pallas import tpu as pltpu
from jax.sharding import PartitionSpec as P

VMEM = pl.BlockSpec(memory_space=pltpu.VMEM)
OCTAVE = 256.0
FULL = 32760.0
SMALLEST = 2.0**-120
SMEM = pl.BlockSpec(memory_space=pltpu.SMEM)


def ring(values, steps):
    reps = lax.axis_size("rep")
    return lax.ppermute(values, "rep", [(i, (i + steps) % reps) for i in range(reps)])


def prepare_lambda(lam_ref, out_ref):
    count = lam_ref.shape[0]
    for tile in range(count):
        out_ref[tile] = lam_ref[tile].T
        out_ref[count + tile] = lam_ref[tile]
    out_ref[2 * count] = jnp.zeros_like(out_ref[2 * count])


def prepare_integrals(start_ref, int_ref, out_ref, turned):
    count, rows, _ = out_ref.shape
    start = pl.multiple_of(start_ref[0], rows)
    for tile in range(count):
        turned[tile] = int_ref[tile].T
        out_ref[tile] = turned[tile, pl.ds(start, rows), :]


def read_tasks(live_ref, mask_ref, task_ref, map_ref, request_ref, code_ref, int_dev, res_tile):
    lam_dev = mask_ref.shape[0]
    task_dev = task_ref.shape[1]
    peers = request_ref.shape[0]
    res_total = map_ref.shape[1]
    placed = map_ref[...]
    parts = jnp.concatenate(
        [placed // res_tile, placed % res_tile, jnp.zeros((6, res_total), jnp.int32)], axis=0
    )
    named = lax.broadcasted_iota(jnp.int32, (res_total, task_dev), 0) == task_ref[2:3, :]
    looked_up = jnp.dot(
        parts.astype(jnp.float32).astype(jnp.bfloat16),
        jnp.where(named, 1.0, 0.0).astype(jnp.bfloat16),
        preferred_element_type=jnp.float32,
    ).astype(jnp.int32)
    o_owner, slot = looked_up[0:1, :], looked_up[1:2, :]
    w_ids = task_ref[1:2, :]
    w_owner, w_local = w_ids // int_dev, w_ids % int_dev
    lam_local = task_ref[0:1, :] % lam_dev
    peer = lax.broadcasted_iota(jnp.int32, (peers, task_dev), 0)
    hits_o = peer == o_owner
    wanted = jnp.where(peer == w_owner, w_local * res_tile, 0) + jnp.where(hits_o, slot, 0)
    wanted = jnp.sum(wanted, axis=1, keepdims=True)
    request_ref[...] = jnp.broadcast_to(wanted, (peers, task_dev)).reshape(request_ref.shape)

    kept = jnp.zeros((1, task_dev), jnp.int32)
    for tile in range(lam_dev):
        kept = jnp.where(lam_local == tile, mask_ref[tile], kept)
    live = lax.broadcasted_iota(jnp.int32, (1, task_dev), 1) < live_ref[0]
    variant = jnp.where((kept == 1) & live, lam_local + lam_dev * task_ref[3:4, :], 2 * lam_dev)
    rows = jnp.concatenate([variant, w_owner, jnp.zeros((6, task_dev), jnp.int32)], axis=0)
    by_owner = lax.dot_general(
        rows.astype(jnp.float32).astype(jnp.bfloat16),
        jnp.where(hits_o, 1.0, 0.0).astype(jnp.bfloat16),
        (((1,), (1,)), ((), ())),
        preferred_element_type=jnp.float32,
    ).astype(jnp.int32)
    code_ref[...] = by_owner[0:1, :] * peers + by_owner[1:2, :]


def pick(request_ref, tiles_ref, out_ref, asked_ref, asked, sem, res_tile):
    peers = out_ref.shape[0]
    got = request_ref[...].reshape(peers, peers)
    diagonal = lax.broadcasted_iota(jnp.int32, got.shape, 0) == lax.broadcasted_iota(jnp.int32, got.shape, 1)
    asked_ref[...] = jnp.sum(jnp.where(diagonal, got, 0), axis=0, keepdims=True)
    copy = pltpu.make_async_copy(asked_ref, asked, sem)
    copy.start()
    copy.wait()

    def body(step, carry):
        for k in range(8):
            peer = step * 8 + k
            out_ref[peer] = tiles_ref[asked[0, peer] // res_tile]
        return carry

    lax.fori_loop(0, peers // 8, body, 0)


def contract(*refs):
    *code_refs, lam_ref, w_ref, out_ref = refs
    peers, rows, edge = w_ref.shape
    unroll = 32

    def one(owner):
        codes = [ref[0, owner] for ref in code_refs]
        left = [w_ref[code % peers] for code in codes]
        right = [lam_ref[code // peers] for code in codes]
        total = jnp.dot(
            jnp.concatenate(left, axis=1),
            jnp.concatenate(right, axis=0),
            preferred_element_type=jnp.float32,
        )
        top = jnp.max(jnp.abs(total), axis=0, keepdims=True)
        scale = jnp.ceil(jnp.log2(jnp.maximum(top, SMALLEST)) * OCTAVE)
        whole = jnp.round(total * (jnp.exp2(scale * (-1.0 / OCTAVE)) * FULL))
        scales = jnp.broadcast_to(scale, (out_ref.shape[1] - rows, edge))
        out_ref[owner] = jnp.concatenate([whole, scales], axis=0).astype(jnp.int32).astype(jnp.int16)

    def body(step, carry):
        for k in range(unroll):
            one(step * unroll + k)
        return carry

    lax.fori_loop(0, peers // unroll, body, 0)


def add_slots(request_ref, x_ref, out_ref, sums):
    slots, rows, _ = out_ref.shape
    sums[...] = jnp.zeros_like(sums)

    def body(step, carry):
        for k in range(4):
            peer = step * 4 + k
            value = x_ref[peer].astype(jnp.int32).astype(jnp.float32)
            scale = jnp.exp2(value[rows:rows + 1] * (1.0 / OCTAVE)) * (1.0 / FULL)
            sums[request_ref[0, peer] % slots] += value[:rows] * scale
        return carry

    lax.fori_loop(0, x_ref.shape[0] // 4, body, 0)
    out_ref[...] = sums[...].astype(out_ref.dtype)


def on_device(lam_tiles, int_tiles, task_list, live_count, tile_mask, owner_map):
    tile_devs = lax.axis_size("tiles")
    reps = lax.axis_size("rep")
    rep_index = lax.axis_index("rep")
    lam_dev, edge, _ = lam_tiles.shape
    int_dev = int_tiles.shape[0]
    res_tile = owner_map.shape[0] // tile_devs
    rows = edge // reps

    request, code = pl.pallas_call(
        functools.partial(read_tasks, int_dev=int_dev, res_tile=res_tile),
        out_shape=(
            jax.ShapeDtypeStruct((tile_devs, 1, 128), jnp.int32),
            jax.ShapeDtypeStruct((1, tile_devs), jnp.int32),
        ),
        in_specs=[SMEM, SMEM, VMEM, VMEM],
        out_specs=(VMEM, VMEM),
        name="read_tasks",
    )(live_count, tile_mask, task_list.T, owner_map[None, :])
    request = lax.all_to_all(request, "tiles", split_axis=0, concat_axis=0, tiled=True)
    codes = [code] + [ring(code, k) for k in range(1, reps)]

    lam_all = pl.pallas_call(
        prepare_lambda,
        out_shape=jax.ShapeDtypeStruct((2 * lam_dev + 1, edge, edge), jnp.bfloat16),
        in_specs=[VMEM],
        out_specs=VMEM,
        name="prepare_lambda",
    )(lam_tiles)
    columns = pl.pallas_call(
        prepare_integrals,
        out_shape=jax.ShapeDtypeStruct((int_dev, rows, edge), jnp.bfloat16),
        in_specs=[SMEM, VMEM],
        out_specs=VMEM,
        scratch_shapes=[pltpu.VMEM((int_dev, edge, edge), jnp.bfloat16)],
        name="prepare_integrals",
    )((rep_index * rows).reshape(1), int_tiles)
    picked, asked = pl.pallas_call(
        functools.partial(pick, res_tile=res_tile),
        out_shape=(
            jax.ShapeDtypeStruct((tile_devs, rows, edge), jnp.bfloat16),
            jax.ShapeDtypeStruct((1, tile_devs), jnp.int32),
        ),
        in_specs=[VMEM, VMEM],
        out_specs=(VMEM, VMEM),
        scratch_shapes=[pltpu.SMEM((1, tile_devs), jnp.int32), pltpu.SemaphoreType.DMA],
        name="pick",
    )(request, columns)
    fetched = lax.all_to_all(picked, "tiles", split_axis=0, concat_axis=0, tiled=True)

    totals = pl.pallas_call(
        contract,
        out_shape=jax.ShapeDtypeStruct((tile_devs, rows + 8, edge), jnp.int16),
        in_specs=[SMEM] * reps + [VMEM, VMEM],
        out_specs=VMEM,
        name="contract",
    )(*codes, lam_all, fetched)
    partial_tiles = lax.all_to_all(totals, "tiles", split_axis=0, concat_axis=0, tiled=True)
    summed = pl.pallas_call(
        add_slots,
        out_shape=jax.ShapeDtypeStruct((res_tile, rows, edge), jnp.bfloat16),
        in_specs=[SMEM, VMEM],
        out_specs=VMEM,
        scratch_shapes=[pltpu.VMEM((res_tile, rows, edge), jnp.float32)],
        name="add_slots",
    )(asked, partial_tiles)
    mine = lax.all_to_all(summed, "rep", split_axis=0, concat_axis=0, tiled=True)
    return mine.reshape(edge, edge).T[None]


def solution(mesh):
    placed = (
        P("tiles", None, None),
        P("tiles", None, None),
        P(("tiles", "rep"), None),
        P(("tiles", "rep")),
        P("tiles"),
        P(),
    )
    return jax.shard_map(
        on_device,
        mesh=mesh,
        in_specs=placed,
        out_specs=P(("tiles", "rep"), None, None),
        check_vma=False,
    )
```

```python
import functools

import jax
import jax.numpy as jnp
from jax import lax
from jax.experimental import pallas as pl
from jax.experimental.pallas import tpu as pltpu
from jax.sharding import PartitionSpec as P

VMEM = pl.BlockSpec(memory_space=pltpu.VMEM)
OCTAVE = 256.0
FULL = 32760.0
SMALLEST = 2.0**-120
ROOM = pltpu.CompilerParams(vmem_limit_bytes=8 * 2**20)
SMEM = pl.BlockSpec(memory_space=pltpu.SMEM)


def ring(values, steps):
    reps = lax.axis_size("rep")
    return lax.ppermute(values, "rep", [(i, (i + steps) % reps) for i in range(reps)])


def prepare_lambda(lam_ref, out_ref):
    count = lam_ref.shape[0]
    for tile in range(count):
        out_ref[tile] = lam_ref[tile].T
        out_ref[count + tile] = lam_ref[tile]
    out_ref[2 * count] = jnp.zeros_like(out_ref[2 * count])


def prepare_integrals(start_ref, int_ref, out_ref, turned):
    count, rows, _ = out_ref.shape
    start = pl.multiple_of(start_ref[0], rows)
    for tile in range(count):
        turned[tile] = int_ref[tile].T
        out_ref[tile] = turned[tile, pl.ds(start, rows), :]


def read_tasks(live_ref, mask_ref, task_ref, map_ref, request_ref, code_ref, int_dev, res_tile):
    lam_dev = mask_ref.shape[0]
    task_dev = task_ref.shape[1]
    peers = request_ref.shape[0]
    res_total = map_ref.shape[1]
    placed = map_ref[...]
    parts = jnp.concatenate(
        [placed // res_tile, placed % res_tile, jnp.zeros((6, res_total), jnp.int32)], axis=0
    )
    named = lax.broadcasted_iota(jnp.int32, (res_total, task_dev), 0) == task_ref[2:3, :]
    looked_up = jnp.dot(
        parts.astype(jnp.float32).astype(jnp.bfloat16),
        jnp.where(named, 1.0, 0.0).astype(jnp.bfloat16),
        preferred_element_type=jnp.float32,
    ).astype(jnp.int32)
    o_owner, slot = looked_up[0:1, :], looked_up[1:2, :]
    w_ids = task_ref[1:2, :]
    w_owner, w_local = w_ids // int_dev, w_ids % int_dev
    lam_local = task_ref[0:1, :] % lam_dev
    peer = lax.broadcasted_iota(jnp.int32, (peers, task_dev), 0)
    hits_o = peer == o_owner
    wanted = jnp.where(peer == w_owner, w_local * res_tile, 0) + jnp.where(hits_o, slot, 0)
    wanted = jnp.sum(wanted, axis=1, keepdims=True)
    request_ref[...] = jnp.broadcast_to(wanted, (peers, task_dev)).reshape(request_ref.shape)

    kept = jnp.zeros((1, task_dev), jnp.int32)
    for tile in range(lam_dev):
        kept = jnp.where(lam_local == tile, mask_ref[tile], kept)
    live = lax.broadcasted_iota(jnp.int32, (1, task_dev), 1) < live_ref[0]
    variant = jnp.where((kept == 1) & live, lam_local + lam_dev * task_ref[3:4, :], 2 * lam_dev)
    rows = jnp.concatenate([variant, w_owner, jnp.zeros((6, task_dev), jnp.int32)], axis=0)
    by_owner = lax.dot_general(
        rows.astype(jnp.float32).astype(jnp.bfloat16),
        jnp.where(hits_o, 1.0, 0.0).astype(jnp.bfloat16),
        (((1,), (1,)), ((), ())),
        preferred_element_type=jnp.float32,
    ).astype(jnp.int32)
    code_ref[...] = by_owner[0:1, :] * peers + by_owner[1:2, :]


def pick(request_ref, tiles_ref, out_ref, asked_ref, asked, sem, res_tile):
    peers = out_ref.shape[0]
    got = request_ref[...].reshape(peers, peers)
    diagonal = lax.broadcasted_iota(jnp.int32, got.shape, 0) == lax.broadcasted_iota(jnp.int32, got.shape, 1)
    asked_ref[...] = jnp.sum(jnp.where(diagonal, got, 0), axis=0, keepdims=True)
    copy = pltpu.make_async_copy(asked_ref, asked, sem)
    copy.start()
    copy.wait()

    def body(step, carry):
        for k in range(8):
            peer = step * 8 + k
            out_ref[peer] = tiles_ref[asked[0, peer] // res_tile]
        return carry

    lax.fori_loop(0, peers // 8, body, 0)


def contract(*refs):
    *code_refs, lam_ref, w_ref, out_ref = refs
    peers, rows, edge = w_ref.shape
    unroll = 64
    words = rows // 2 + 1

    def one(step, place):
        owner = step * unroll + place
        codes = [ref[0, owner] for ref in code_refs]
        left = [w_ref[code % peers] for code in codes]
        right = [lam_ref[code // peers] for code in codes]
        total = jnp.dot(
            jnp.concatenate(left, axis=1),
            jnp.concatenate(right, axis=0),
            preferred_element_type=jnp.float32,
        )
        top = jnp.max(jnp.abs(total), axis=0, keepdims=True)
        scale = jnp.ceil(jnp.log2(jnp.maximum(top, SMALLEST)) * OCTAVE)
        whole = jnp.round(total * (jnp.exp2(scale * (-1.0 / OCTAVE)) * FULL)).astype(jnp.int32)
        first = pl.multiple_of(step * unroll * words, 8) + place * words
        out_ref[pl.ds(first, rows // 2), :] = whole[: rows // 2] * 65536 + whole[rows // 2 :]
        out_ref[pl.ds(first + rows // 2, 1), :] = scale.astype(jnp.int32)

    def body(step, carry):
        for k in range(unroll):
            one(step, k)
        return carry

    lax.fori_loop(0, peers // unroll, body, 0)


def add_slots(request_ref, x_ref, out_ref, sums):
    slots, rows, _ = out_ref.shape
    words = rows // 2 + 1
    unroll = 8
    sums[...] = jnp.zeros_like(sums)

    def body(step, carry):
        for k in range(unroll):
            first = pl.multiple_of(step * unroll * words, 8) + k * words
            pairs = x_ref[pl.ds(first, rows // 2), :]
            low = lax.shift_right_arithmetic(lax.shift_left(pairs, 16), 16)
            high = lax.shift_right_arithmetic(pairs - low, 16)
            scale = x_ref[pl.ds(first + rows // 2, 1), :].astype(jnp.float32)
            scale = jnp.exp2(scale * (1.0 / OCTAVE)) * (1.0 / FULL)
            value = jnp.concatenate([high, low], axis=0).astype(jnp.float32) * scale
            sums[request_ref[0, step * unroll + k] % slots] += value
        return carry

    lax.fori_loop(0, request_ref.shape[1] // unroll, body, 0)
    out_ref[...] = sums[...].astype(out_ref.dtype)


def on_device(lam_tiles, int_tiles, task_list, live_count, tile_mask, owner_map):
    tile_devs = lax.axis_size("tiles")
    reps = lax.axis_size("rep")
    rep_index = lax.axis_index("rep")
    lam_dev, edge, _ = lam_tiles.shape
    int_dev = int_tiles.shape[0]
    res_tile = owner_map.shape[0] // tile_devs
    rows = edge // reps
    words = rows // 2 + 1

    request, code = pl.pallas_call(
        functools.partial(read_tasks, int_dev=int_dev, res_tile=res_tile),
        out_shape=(
            jax.ShapeDtypeStruct((tile_devs, 1, 128), jnp.int32),
            jax.ShapeDtypeStruct((1, tile_devs), jnp.int32),
        ),
        in_specs=[SMEM, SMEM, VMEM, VMEM],
        out_specs=(VMEM, VMEM),
        name="read_tasks",
    )(live_count, tile_mask, task_list.T, owner_map[None, :])
    request = lax.all_to_all(request, "tiles", split_axis=0, concat_axis=0, tiled=True)
    codes = [code] + [ring(code, k) for k in range(1, reps)]

    lam_all = pl.pallas_call(
        prepare_lambda,
        out_shape=jax.ShapeDtypeStruct((2 * lam_dev + 1, edge, edge), jnp.bfloat16),
        in_specs=[VMEM],
        out_specs=VMEM,
        compiler_params=ROOM,
        name="prepare_lambda",
    )(lam_tiles)
    columns = pl.pallas_call(
        prepare_integrals,
        out_shape=jax.ShapeDtypeStruct((int_dev, rows, edge), jnp.bfloat16),
        in_specs=[SMEM, VMEM],
        out_specs=VMEM,
        scratch_shapes=[pltpu.VMEM((int_dev, edge, edge), jnp.bfloat16)],
        compiler_params=ROOM,
        name="prepare_integrals",
    )((rep_index * rows).reshape(1), int_tiles)
    picked, asked = pl.pallas_call(
        functools.partial(pick, res_tile=res_tile),
        out_shape=(
            jax.ShapeDtypeStruct((tile_devs, rows, edge), jnp.bfloat16),
            jax.ShapeDtypeStruct((1, tile_devs), jnp.int32),
        ),
        in_specs=[VMEM, VMEM],
        out_specs=(VMEM, VMEM),
        scratch_shapes=[pltpu.SMEM((1, tile_devs), jnp.int32), pltpu.SemaphoreType.DMA],
        compiler_params=ROOM,
        name="pick",
    )(request, columns)
    fetched = lax.all_to_all(picked, "tiles", split_axis=0, concat_axis=0, tiled=True)

    totals = pl.pallas_call(
        contract,
        out_shape=jax.ShapeDtypeStruct((tile_devs * words, edge), jnp.int32),
        in_specs=[SMEM] * reps + [VMEM, VMEM],
        out_specs=VMEM,
        compiler_params=ROOM,
        name="contract",
    )(*codes, lam_all, fetched)
    totals = totals.reshape(tile_devs, words, 1, edge)
    partial_tiles = lax.all_to_all(totals, "tiles", split_axis=0, concat_axis=0, tiled=True)
    partial_tiles = partial_tiles.reshape(tile_devs * words, edge)
    summed = pl.pallas_call(
        add_slots,
        out_shape=jax.ShapeDtypeStruct((res_tile, rows, edge), jnp.bfloat16),
        in_specs=[SMEM, VMEM],
        out_specs=VMEM,
        scratch_shapes=[pltpu.VMEM((res_tile, rows, edge), jnp.float32)],
        compiler_params=ROOM,
        name="add_slots",
    )(asked, partial_tiles)
    mine = lax.all_to_all(summed, "rep", split_axis=0, concat_axis=0, tiled=True)
    return mine.reshape(edge, edge).T[None]


def solution(mesh):
    placed = (
        P("tiles", None, None),
        P("tiles", None, None),
        P(("tiles", "rep"), None),
        P(("tiles", "rep")),
        P("tiles"),
        P(),
    )
    return jax.shard_map(
        on_device,
        mesh=mesh,
        in_specs=placed,
        out_specs=P(("tiles", "rep"), None, None),
        check_vma=False,
    )
```

```python
import functools

import jax
import jax.numpy as jnp
from jax import lax
from jax.experimental import pallas as pl
from jax.experimental.pallas import tpu as pltpu
from jax.sharding import PartitionSpec as P

VMEM = pl.BlockSpec(memory_space=pltpu.VMEM)
OCTAVE = 256.0
FULL = 32760.0
SMALLEST = 2.0**-120
ROOM = pltpu.CompilerParams(vmem_limit_bytes=8 * 2**20)
SMEM = pl.BlockSpec(memory_space=pltpu.SMEM)


def power(size):
    return size.bit_length() - 1


def ring(values, steps):
    reps = lax.axis_size("rep")
    return lax.ppermute(values, "rep", [(i, (i + steps) % reps) for i in range(reps)])


def prepare_lambda(lam_ref, out_ref):
    count = lam_ref.shape[0]
    for tile in range(count):
        out_ref[tile] = lam_ref[tile].T
        out_ref[count + tile] = lam_ref[tile]
    out_ref[2 * count] = jnp.zeros_like(out_ref[2 * count])


def prepare_integrals(start_ref, int_ref, out_ref, turned):
    count, rows, _ = out_ref.shape
    start = pl.multiple_of(start_ref[0], rows)
    for tile in range(count):
        turned[tile] = int_ref[tile].T
        out_ref[tile] = turned[tile, pl.ds(start, rows), :]


def read_tasks(live_ref, mask_ref, task_ref, map_ref, request_ref, code_ref, int_dev, res_tile):
    lam_dev = mask_ref.shape[0]
    task_dev = task_ref.shape[1]
    peers = request_ref.shape[0]
    res_total = map_ref.shape[1]
    placed = map_ref[...]
    parts = jnp.concatenate(
        [placed // res_tile, placed % res_tile, jnp.zeros((6, res_total), jnp.int32)], axis=0
    )
    named = lax.broadcasted_iota(jnp.int32, (res_total, task_dev), 0) == task_ref[2:3, :]
    looked_up = jnp.dot(
        parts.astype(jnp.float32).astype(jnp.bfloat16),
        jnp.where(named, 1.0, 0.0).astype(jnp.bfloat16),
        preferred_element_type=jnp.float32,
    ).astype(jnp.int32)
    o_owner, slot = looked_up[0:1, :], looked_up[1:2, :]
    w_ids = task_ref[1:2, :]
    w_owner, w_local = w_ids // int_dev, w_ids % int_dev
    lam_local = task_ref[0:1, :] % lam_dev
    peer = lax.broadcasted_iota(jnp.int32, (peers, task_dev), 0)
    hits_o = peer == o_owner
    wanted = jnp.where(peer == w_owner, w_local * res_tile, 0) + jnp.where(hits_o, slot, 0)
    wanted = jnp.sum(wanted, axis=1, keepdims=True)
    request_ref[...] = jnp.broadcast_to(wanted, (peers, task_dev)).reshape(request_ref.shape)

    kept = jnp.zeros((1, task_dev), jnp.int32)
    for tile in range(lam_dev):
        kept = jnp.where(lam_local == tile, mask_ref[tile], kept)
    live = lax.broadcasted_iota(jnp.int32, (1, task_dev), 1) < live_ref[0]
    variant = jnp.where((kept == 1) & live, lam_local + lam_dev * task_ref[3:4, :], 2 * lam_dev)
    rows = jnp.concatenate([variant, w_owner, jnp.zeros((6, task_dev), jnp.int32)], axis=0)
    by_owner = lax.dot_general(
        rows.astype(jnp.float32).astype(jnp.bfloat16),
        jnp.where(hits_o, 1.0, 0.0).astype(jnp.bfloat16),
        (((1,), (1,)), ((), ())),
        preferred_element_type=jnp.float32,
    ).astype(jnp.int32)
    code_ref[...] = by_owner[0:1, :] * peers + by_owner[1:2, :]


def pick(request_ref, tiles_ref, out_ref, asked_ref, asked, sem, res_tile):
    peers = out_ref.shape[0]
    got = request_ref[...].reshape(peers, peers)
    diagonal = lax.broadcasted_iota(jnp.int32, got.shape, 0) == lax.broadcasted_iota(jnp.int32, got.shape, 1)
    asked_ref[...] = jnp.sum(jnp.where(diagonal, got, 0), axis=0, keepdims=True)
    copy = pltpu.make_async_copy(asked_ref, asked, sem)
    copy.start()
    copy.wait()

    def body(step, carry):
        for k in range(32):
            peer = step * 32 + k
            out_ref[peer] = tiles_ref[lax.shift_right_logical(asked[0, peer], power(res_tile))]
        return carry

    lax.fori_loop(0, peers // 32, body, 0)


def contract(*refs):
    *code_refs, lam_ref, w_ref, out_ref = refs
    peers, rows, edge = w_ref.shape
    unroll = 64
    words = rows // 2 + 1

    def one(step, place):
        owner = step * unroll + place
        codes = [ref[0, owner] for ref in code_refs]
        left = [w_ref[lax.bitwise_and(code, peers - 1)] for code in codes]
        right = [lam_ref[lax.shift_right_logical(code, power(peers))] for code in codes]
        total = jnp.dot(
            jnp.concatenate(left, axis=1),
            jnp.concatenate(right, axis=0),
            preferred_element_type=jnp.float32,
        )
        top = jnp.max(jnp.abs(total), axis=0, keepdims=True)
        scale = jnp.ceil(jnp.log2(jnp.maximum(top, SMALLEST)) * OCTAVE)
        whole = jnp.round(total * (jnp.exp2(scale * (-1.0 / OCTAVE)) * FULL)).astype(jnp.int32)
        first = pl.multiple_of(step * unroll * words, 8) + place * words
        out_ref[pl.ds(first, rows // 2), :] = whole[: rows // 2] * 65536 + whole[rows // 2 :]
        out_ref[pl.ds(first + rows // 2, 1), :] = scale.astype(jnp.int32)

    def body(step, carry):
        for k in range(unroll):
            one(step, k)
        return carry

    lax.fori_loop(0, peers // unroll, body, 0)


def add_slots(request_ref, x_ref, out_ref, sums):
    slots, rows, _ = out_ref.shape
    words = rows // 2 + 1
    unroll = 8
    sums[...] = jnp.zeros_like(sums)

    def body(step, carry):
        for k in range(unroll):
            first = pl.multiple_of(step * unroll * words, 8) + k * words
            pairs = x_ref[pl.ds(first, rows // 2), :]
            low = lax.shift_right_arithmetic(lax.shift_left(pairs, 16), 16)
            high = lax.shift_right_arithmetic(pairs - low, 16)
            scale = x_ref[pl.ds(first + rows // 2, 1), :].astype(jnp.float32)
            scale = jnp.exp2(scale * (1.0 / OCTAVE)) * (1.0 / FULL)
            value = jnp.concatenate([high, low], axis=0).astype(jnp.float32) * scale
            slot = lax.bitwise_and(request_ref[0, step * unroll + k], slots - 1)
            sums[slot] += value
        return carry

    lax.fori_loop(0, request_ref.shape[1] // unroll, body, 0)
    out_ref[...] = sums[...].astype(out_ref.dtype)


def on_device(lam_tiles, int_tiles, task_list, live_count, tile_mask, owner_map):
    tile_devs = lax.axis_size("tiles")
    reps = lax.axis_size("rep")
    rep_index = lax.axis_index("rep")
    lam_dev, edge, _ = lam_tiles.shape
    int_dev = int_tiles.shape[0]
    res_tile = owner_map.shape[0] // tile_devs
    rows = edge // reps
    words = rows // 2 + 1

    request, code = pl.pallas_call(
        functools.partial(read_tasks, int_dev=int_dev, res_tile=res_tile),
        out_shape=(
            jax.ShapeDtypeStruct((tile_devs, 1, 128), jnp.int32),
            jax.ShapeDtypeStruct((1, tile_devs), jnp.int32),
        ),
        in_specs=[SMEM, SMEM, VMEM, VMEM],
        out_specs=(VMEM, VMEM),
        name="read_tasks",
    )(live_count, tile_mask, task_list.T, owner_map[None, :])
    request = lax.all_to_all(request, "tiles", split_axis=0, concat_axis=0, tiled=True)
    codes = [code] + [ring(code, k) for k in range(1, reps)]

    lam_all = pl.pallas_call(
        prepare_lambda,
        out_shape=jax.ShapeDtypeStruct((2 * lam_dev + 1, edge, edge), jnp.bfloat16),
        in_specs=[VMEM],
        out_specs=VMEM,
        compiler_params=ROOM,
        name="prepare_lambda",
    )(lam_tiles)
    columns = pl.pallas_call(
        prepare_integrals,
        out_shape=jax.ShapeDtypeStruct((int_dev, rows, edge), jnp.bfloat16),
        in_specs=[SMEM, VMEM],
        out_specs=VMEM,
        scratch_shapes=[pltpu.VMEM((int_dev, edge, edge), jnp.bfloat16)],
        compiler_params=ROOM,
        name="prepare_integrals",
    )((rep_index * rows).reshape(1), int_tiles)
    picked, asked = pl.pallas_call(
        functools.partial(pick, res_tile=res_tile),
        out_shape=(
            jax.ShapeDtypeStruct((tile_devs, rows, edge), jnp.bfloat16),
            jax.ShapeDtypeStruct((1, tile_devs), jnp.int32),
        ),
        in_specs=[VMEM, VMEM],
        out_specs=(VMEM, VMEM),
        scratch_shapes=[pltpu.SMEM((1, tile_devs), jnp.int32), pltpu.SemaphoreType.DMA],
        compiler_params=ROOM,
        name="pick",
    )(request, columns)
    fetched = lax.all_to_all(picked, "tiles", split_axis=0, concat_axis=0, tiled=True)

    totals = pl.pallas_call(
        contract,
        out_shape=jax.ShapeDtypeStruct((tile_devs * words, edge), jnp.int32),
        in_specs=[SMEM] * reps + [VMEM, VMEM],
        out_specs=VMEM,
        compiler_params=ROOM,
        name="contract",
    )(*codes, lam_all, fetched)
    totals = totals.reshape(tile_devs, words, 1, edge)
    partial_tiles = lax.all_to_all(totals, "tiles", split_axis=0, concat_axis=0, tiled=True)
    partial_tiles = partial_tiles.reshape(tile_devs * words, edge)
    summed = pl.pallas_call(
        add_slots,
        out_shape=jax.ShapeDtypeStruct((res_tile, rows, edge), jnp.bfloat16),
        in_specs=[SMEM, VMEM],
        out_specs=VMEM,
        scratch_shapes=[pltpu.VMEM((res_tile, rows, edge), jnp.float32)],
        compiler_params=ROOM,
        name="add_slots",
    )(asked, partial_tiles)
    mine = lax.all_to_all(summed, "rep", split_axis=0, concat_axis=0, tiled=True)
    return mine.reshape(edge, edge).T[None]


def solution(mesh):
    placed = (
        P("tiles", None, None),
        P("tiles", None, None),
        P(("tiles", "rep"), None),
        P(("tiles", "rep")),
        P("tiles"),
        P(),
    )
    return jax.shard_map(
        on_device,
        mesh=mesh,
        in_specs=placed,
        out_specs=P(("tiles", "rep"), None, None),
        check_vma=False,
    )
```

```python
import functools

import jax
import jax.numpy as jnp
from jax import lax
from jax.experimental import pallas as pl
from jax.experimental.pallas import tpu as pltpu
from jax.sharding import PartitionSpec as P

VMEM = pl.BlockSpec(memory_space=pltpu.VMEM)
OCTAVE = 256.0
FULL = 32760.0
SMALLEST = 2.0**-110
ROOM = pltpu.CompilerParams(vmem_limit_bytes=8 * 2**20)
SMEM = pl.BlockSpec(memory_space=pltpu.SMEM)


def power(size):
    return size.bit_length() - 1


def ring(values, steps):
    reps = lax.axis_size("rep")
    return lax.ppermute(values, "rep", [(i, (i + steps) % reps) for i in range(reps)])


def prepare_lambda(lam_ref, out_ref):
    count = lam_ref.shape[0]
    for tile in range(count):
        out_ref[tile] = lam_ref[tile].T
        out_ref[count + tile] = lam_ref[tile]
    out_ref[2 * count] = jnp.zeros_like(out_ref[2 * count])


def prepare_integrals(start_ref, int_ref, out_ref, turned):
    count, rows, _ = out_ref.shape
    start = pl.multiple_of(start_ref[0], rows)
    for tile in range(count):
        turned[tile] = int_ref[tile].T
        out_ref[tile] = turned[tile, pl.ds(start, rows), :]


def ask(tasks, request_ref, int_dev):
    peers, task_dev = request_ref.shape[0], tasks.shape[1]
    w_ids = tasks[1:2, :]
    peer = lax.broadcasted_iota(jnp.int32, (peers, task_dev), 0)
    wanted = jnp.where(peer == lax.shift_right_logical(w_ids, power(int_dev)), w_ids, 0)
    wanted = jnp.sum(lax.bitwise_and(wanted, int_dev - 1), axis=1, keepdims=True)
    request_ref[...] = jnp.broadcast_to(wanted, (peers, task_dev))


def read_tasks(live_ref, mask_ref, task_ref, map_ref, code_ref, int_dev, res_tile):
    lam_dev = mask_ref.shape[0]
    task_dev = task_ref.shape[1]
    peers = code_ref.shape[1]
    res_total = map_ref.shape[1]
    placed = map_ref[...]
    parts = jnp.concatenate(
        [placed // res_tile, placed % res_tile, jnp.zeros((6, res_total), jnp.int32)], axis=0
    )
    named = lax.broadcasted_iota(jnp.int32, (res_total, task_dev), 0) == task_ref[2:3, :]
    looked_up = jnp.dot(
        parts.astype(jnp.float32).astype(jnp.bfloat16),
        jnp.where(named, 1.0, 0.0).astype(jnp.bfloat16),
        preferred_element_type=jnp.float32,
    ).astype(jnp.int32)
    o_owner, slot = looked_up[0:1, :], looked_up[1:2, :]
    w_owner = task_ref[1:2, :] // int_dev
    lam_local = task_ref[0:1, :] % lam_dev
    hits_o = lax.broadcasted_iota(jnp.int32, (peers, task_dev), 0) == o_owner
    kept = jnp.zeros((1, task_dev), jnp.int32)
    for tile in range(lam_dev):
        kept = jnp.where(lam_local == tile, mask_ref[tile], kept)
    live = lax.broadcasted_iota(jnp.int32, (1, task_dev), 1) < live_ref[0]
    variant = jnp.where((kept == 1) & live, lam_local + lam_dev * task_ref[3:4, :], 2 * lam_dev)
    rows = jnp.concatenate([variant, w_owner, slot, jnp.zeros((5, task_dev), jnp.int32)], axis=0)
    by_owner = lax.dot_general(
        rows.astype(jnp.float32).astype(jnp.bfloat16),
        jnp.where(hits_o, 1.0, 0.0).astype(jnp.bfloat16),
        (((1,), (1,)), ((), ())),
        preferred_element_type=jnp.float32,
    ).astype(jnp.int32)
    code_ref[...] = (by_owner[0:1, :] * peers + by_owner[1:2, :]) * res_tile + by_owner[2:3, :]


def pick(request_ref, tiles_ref, out_ref, row, asked, sem):
    peers = out_ref.shape[0]
    got = request_ref[...]
    diagonal = lax.broadcasted_iota(jnp.int32, got.shape, 0) == lax.broadcasted_iota(jnp.int32, got.shape, 1)
    row[...] = jnp.sum(jnp.where(diagonal, got, 0), axis=0, keepdims=True)
    copy = pltpu.make_async_copy(row, asked, sem)
    copy.start()
    copy.wait()

    def body(step, carry):
        for k in range(32):
            peer = step * 32 + k
            out_ref[peer] = tiles_ref[asked[0, peer]]
        return carry

    lax.fori_loop(0, peers // 32, body, 0)


def contract(*refs, slots):
    *code_refs, lam_ref, w_ref, out_ref = refs
    peers, rows, edge = w_ref.shape
    unroll = 64
    words = rows // 2 + 1

    def one(step, place):
        owner = step * unroll + place
        codes = [ref[0, owner] for ref in code_refs]
        slot = lax.bitwise_and(codes[0], slots - 1)
        codes = [lax.shift_right_logical(code, power(slots)) for code in codes]
        left = [w_ref[lax.bitwise_and(code, peers - 1)] for code in codes]
        right = [lam_ref[lax.shift_right_logical(code, power(peers))] for code in codes]
        total = jnp.dot(
            jnp.concatenate(left, axis=1),
            jnp.concatenate(right, axis=0),
            preferred_element_type=jnp.float32,
        )
        top = jnp.max(jnp.abs(total), axis=0, keepdims=True)
        scale = jnp.ceil(jnp.log2(jnp.maximum(top, SMALLEST)) * OCTAVE)
        whole = jnp.round(total * (jnp.exp2(scale * (-1.0 / OCTAVE)) * FULL)).astype(jnp.int32)
        first = pl.multiple_of(step * unroll * words, 8) + place * words
        out_ref[pl.ds(first, rows // 2), :] = whole[: rows // 2] * 65536 + whole[rows // 2 :]
        out_ref[pl.ds(first + rows // 2, 1), :] = scale.astype(jnp.int32) * slots + slot

    def body(step, carry):
        for k in range(unroll):
            one(step, k)
        return carry

    lax.fori_loop(0, peers // unroll, body, 0)


def add_slots(x_ref, out_ref):
    slots, rows, edge = out_ref.shape
    words = rows // 2 + 1
    unroll = 16

    def body(step, sums):
        for k in range(unroll):
            first = pl.multiple_of(step * unroll * words, 8) + k * words
            pairs = x_ref[pl.ds(first, rows // 2), :]
            low = lax.shift_right_arithmetic(lax.shift_left(pairs, 16), 16)
            high = lax.shift_right_arithmetic(pairs - low, 16)
            last = x_ref[pl.ds(first + rows // 2, 1), :]
            slot = lax.bitwise_and(last, slots - 1)
            scale = lax.shift_right_arithmetic(last, power(slots)).astype(jnp.float32)
            scale = jnp.exp2(scale * (1.0 / OCTAVE)) * (1.0 / FULL)
            value = jnp.concatenate([high, low], axis=0).astype(jnp.float32) * scale
            mine = [jnp.broadcast_to(slot, (rows, edge)) == s for s in range(slots)]
            sums = tuple(jnp.where(m, total + value, total) for m, total in zip(mine, sums))
        return sums

    zero = jnp.zeros((rows, edge), jnp.float32)
    sums = lax.fori_loop(0, x_ref.shape[0] // (words * unroll), body, (zero,) * slots)
    for s in range(slots):
        out_ref[s] = sums[s].astype(out_ref.dtype)


def on_device(lam_tiles, int_tiles, task_list, live_count, tile_mask, owner_map):
    tile_devs = lax.axis_size("tiles")
    reps = lax.axis_size("rep")
    rep_index = lax.axis_index("rep")
    lam_dev, edge, _ = lam_tiles.shape
    int_dev = int_tiles.shape[0]
    res_tile = owner_map.shape[0] // tile_devs
    rows = edge // reps
    words = rows // 2 + 1

    tasks = task_list.T
    request = pl.pallas_call(
        functools.partial(ask, int_dev=int_dev),
        out_shape=jax.ShapeDtypeStruct((tile_devs, 128), jnp.int32),
        in_specs=[VMEM],
        out_specs=VMEM,
        compiler_params=ROOM,
        name="ask",
    )(tasks)
    request = lax.all_to_all(
        request.reshape(tile_devs, 1, 128), "tiles", split_axis=0, concat_axis=0, tiled=True
    ).reshape(tile_devs, 128)
    code = pl.pallas_call(
        functools.partial(read_tasks, int_dev=int_dev, res_tile=res_tile),
        out_shape=jax.ShapeDtypeStruct((1, tile_devs), jnp.int32),
        in_specs=[SMEM, SMEM, VMEM, VMEM],
        out_specs=VMEM,
        name="read_tasks",
    )(live_count, tile_mask, tasks, owner_map[None, :])
    codes = [code] + [ring(code, k) for k in range(1, reps)]

    lam_all = pl.pallas_call(
        prepare_lambda,
        out_shape=jax.ShapeDtypeStruct((2 * lam_dev + 1, edge, edge), jnp.bfloat16),
        in_specs=[VMEM],
        out_specs=VMEM,
        compiler_params=ROOM,
        name="prepare_lambda",
    )(lam_tiles)
    columns = pl.pallas_call(
        prepare_integrals,
        out_shape=jax.ShapeDtypeStruct((int_dev, rows, edge), jnp.bfloat16),
        in_specs=[SMEM, VMEM],
        out_specs=VMEM,
        scratch_shapes=[pltpu.VMEM((int_dev, edge, edge), jnp.bfloat16)],
        compiler_params=ROOM,
        name="prepare_integrals",
    )((rep_index * rows).reshape(1), int_tiles)
    picked = pl.pallas_call(
        pick,
        out_shape=jax.ShapeDtypeStruct((tile_devs, rows, edge), jnp.bfloat16),
        in_specs=[VMEM, VMEM],
        out_specs=VMEM,
        scratch_shapes=[
            pltpu.VMEM((1, tile_devs), jnp.int32),
            pltpu.SMEM((1, tile_devs), jnp.int32),
            pltpu.SemaphoreType.DMA,
        ],
        compiler_params=ROOM,
        name="pick",
    )(request, columns)
    fetched = lax.all_to_all(picked, "tiles", split_axis=0, concat_axis=0, tiled=True)

    totals = pl.pallas_call(
        functools.partial(contract, slots=res_tile),
        out_shape=jax.ShapeDtypeStruct((tile_devs * words, edge), jnp.int32),
        in_specs=[SMEM] * reps + [VMEM, VMEM],
        out_specs=VMEM,
        compiler_params=ROOM,
        name="contract",
    )(*codes, lam_all, fetched)
    totals = totals.reshape(tile_devs, words, 1, edge)
    partial_tiles = lax.all_to_all(totals, "tiles", split_axis=0, concat_axis=0, tiled=True)
    partial_tiles = partial_tiles.reshape(tile_devs * words, edge)
    summed = pl.pallas_call(
        add_slots,
        out_shape=jax.ShapeDtypeStruct((res_tile, rows, edge), jnp.bfloat16),
        in_specs=[VMEM],
        out_specs=VMEM,
        compiler_params=ROOM,
        name="add_slots",
    )(partial_tiles)
    mine = lax.all_to_all(summed, "rep", split_axis=0, concat_axis=0, tiled=True)
    return mine.reshape(edge, edge).T[None]


def solution(mesh):
    placed = (
        P("tiles", None, None),
        P("tiles", None, None),
        P(("tiles", "rep"), None),
        P(("tiles", "rep")),
        P("tiles"),
        P(),
    )
    return jax.shard_map(
        on_device,
        mesh=mesh,
        in_specs=placed,
        out_specs=P(("tiles", "rep"), None, None),
        check_vma=False,
    )
```

```python
import functools

import jax
import jax.numpy as jnp
from jax import lax
from jax.experimental import pallas as pl
from jax.experimental.pallas import tpu as pltpu
from jax.sharding import PartitionSpec as P

VMEM = pl.BlockSpec(memory_space=pltpu.VMEM)
OCTAVE = 256.0
FULL = 32760.0
SMALLEST = 2.0**-110
ROOM = pltpu.CompilerParams(vmem_limit_bytes=8 * 2**20)
SMEM = pl.BlockSpec(memory_space=pltpu.SMEM)


def power(size):
    return size.bit_length() - 1


def ring(values, steps):
    reps = lax.axis_size("rep")
    return lax.ppermute(values, "rep", [(i, (i + steps) % reps) for i in range(reps)])


def prepare_lambda(lam_ref, out_ref):
    count = lam_ref.shape[0]
    for tile in range(count):
        out_ref[tile] = lam_ref[tile].T
        out_ref[count + tile] = lam_ref[tile]
    out_ref[2 * count] = jnp.zeros_like(out_ref[2 * count])


def prepare_integrals(place_ref, own_ref, other_ref, out_ref, turned):
    _, count, rows, _ = out_ref.shape
    core = place_ref[0]
    start = pl.multiple_of(place_ref[1], rows)
    for place, tiles in ((core, own_ref), (1 - core, other_ref)):
        for tile in range(count):
            turned[tile] = tiles[tile].T
            out_ref[place, tile] = turned[tile, pl.ds(start, rows), :]


def ask(task_ref, request_ref, int_dev):
    peers, task_dev = request_ref.shape[0], task_ref.shape[1]
    w_ids = task_ref[1:2, :]
    w_owner = lax.shift_right_logical(w_ids, power(int_dev))
    place = lax.bitwise_and(w_owner, 1) * power(int_dev)
    named = lax.shift_left(lax.bitwise_and(w_ids, int_dev - 1), place)
    peer = lax.broadcasted_iota(jnp.int32, (peers, task_dev), 0)
    wanted = jnp.where(peer == lax.shift_right_logical(w_owner, 1), named, 0)
    wanted = jnp.sum(wanted, axis=1, keepdims=True)
    request_ref[...] = jnp.broadcast_to(wanted, (peers, task_dev))


def read_tasks(live_ref, mask_ref, task_ref, map_ref, code_ref, int_dev, res_tile):
    lam_dev = mask_ref.shape[0]
    task_dev = task_ref.shape[1]
    peers = code_ref.shape[1]
    res_total = map_ref.shape[1]
    placed = map_ref[...]
    parts = jnp.concatenate(
        [placed // res_tile, placed % res_tile, jnp.zeros((6, res_total), jnp.int32)], axis=0
    )
    named = lax.broadcasted_iota(jnp.int32, (res_total, task_dev), 0) == task_ref[2:3, :]
    looked_up = jnp.dot(
        parts.astype(jnp.float32).astype(jnp.bfloat16),
        jnp.where(named, 1.0, 0.0).astype(jnp.bfloat16),
        preferred_element_type=jnp.float32,
    ).astype(jnp.int32)
    o_owner, slot = looked_up[0:1, :], looked_up[1:2, :]
    w_owner = task_ref[1:2, :] // int_dev
    lam_local = task_ref[0:1, :] % lam_dev
    hits_o = lax.broadcasted_iota(jnp.int32, (peers, task_dev), 0) == o_owner
    kept = jnp.zeros((1, task_dev), jnp.int32)
    for tile in range(lam_dev):
        kept = jnp.where(lam_local == tile, mask_ref[tile], kept)
    live = lax.broadcasted_iota(jnp.int32, (1, task_dev), 1) < live_ref[0]
    variant = jnp.where((kept == 1) & live, lam_local + lam_dev * task_ref[3:4, :], 2 * lam_dev)
    rows = jnp.concatenate([variant, w_owner, slot, jnp.zeros((5, task_dev), jnp.int32)], axis=0)
    by_owner = lax.dot_general(
        rows.astype(jnp.float32).astype(jnp.bfloat16),
        jnp.where(hits_o, 1.0, 0.0).astype(jnp.bfloat16),
        (((1,), (1,)), ((), ())),
        preferred_element_type=jnp.float32,
    ).astype(jnp.int32)
    code_ref[...] = (by_owner[0:1, :] * peers + by_owner[1:2, :]) * res_tile + by_owner[2:3, :]


def pick(request_ref, tiles_ref, out_ref, row, asked, sem):
    peers, both, edge = out_ref.shape
    _, int_dev, rows, _ = tiles_ref.shape
    got = request_ref[...]
    diagonal = lax.broadcasted_iota(jnp.int32, got.shape, 0) == lax.broadcasted_iota(jnp.int32, got.shape, 1)
    row[...] = jnp.sum(jnp.where(diagonal, got, 0), axis=0, keepdims=True)
    copy = pltpu.make_async_copy(row, asked, sem)
    copy.start()
    copy.wait()

    def body(step, carry):
        for k in range(16):
            peer = step * 16 + k
            word = asked[0, peer]
            out_ref[peer, :rows] = tiles_ref[0, lax.bitwise_and(word, int_dev - 1)]
            out_ref[peer, rows:] = tiles_ref[1, lax.shift_right_logical(word, power(int_dev))]
        return carry

    lax.fori_loop(0, peers // 16, body, 0)


def contract(*refs, slots):
    *code_refs, lam_ref, w_ref, out_ref = refs
    peers, rows, edge = w_ref.shape
    unroll = 64
    words = rows // 2 + 1

    def one(step, place):
        owner = step * unroll + place
        codes = [ref[0, owner] for ref in code_refs]
        slot = lax.bitwise_and(codes[0], slots - 1)
        codes = [lax.shift_right_logical(code, power(slots)) for code in codes]
        left = [w_ref[lax.bitwise_and(code, peers - 1)] for code in codes]
        right = [lam_ref[lax.shift_right_logical(code, power(peers))] for code in codes]
        total = jnp.dot(
            jnp.concatenate(left, axis=1),
            jnp.concatenate(right, axis=0),
            preferred_element_type=jnp.float32,
        )
        top = jnp.max(jnp.abs(total), axis=0, keepdims=True)
        scale = jnp.ceil(jnp.log2(jnp.maximum(top, SMALLEST)) * OCTAVE)
        whole = jnp.round(total * (jnp.exp2(scale * (-1.0 / OCTAVE)) * FULL)).astype(jnp.int32)
        first = pl.multiple_of(step * unroll * words, 8) + place * words
        out_ref[pl.ds(first, rows // 2), :] = whole[: rows // 2] * 65536 + whole[rows // 2 :]
        out_ref[pl.ds(first + rows // 2, 1), :] = scale.astype(jnp.int32) * slots + slot

    def body(step, carry):
        for k in range(unroll):
            one(step, k)
        return carry

    lax.fori_loop(0, peers // unroll, body, 0)


def add_slots(x_ref, out_ref):
    owners, slots, rows, edge = out_ref.shape
    words = rows // 2 + 1
    unroll = 16
    zero = jnp.zeros((rows, edge), jnp.float32)
    for owner in range(owners):

        def body(step, sums):
            for k in range(unroll):
                first = pl.multiple_of(step * unroll * owners * words, 8) + (k * owners + owner) * words
                pairs = x_ref[pl.ds(first, rows // 2), :]
                low = lax.shift_right_arithmetic(lax.shift_left(pairs, 16), 16)
                high = lax.shift_right_arithmetic(pairs - low, 16)
                last = x_ref[pl.ds(first + rows // 2, 1), :]
                slot = lax.bitwise_and(last, slots - 1)
                scale = lax.shift_right_arithmetic(last, power(slots)).astype(jnp.float32)
                scale = jnp.exp2(scale * (1.0 / OCTAVE)) * (1.0 / FULL)
                value = jnp.concatenate([high, low], axis=0).astype(jnp.float32) * scale
                mine = [jnp.broadcast_to(slot, (rows, edge)) == s for s in range(slots)]
                sums = tuple(jnp.where(m, total + value, total) for m, total in zip(mine, sums))
            return sums

        sums = lax.fori_loop(0, x_ref.shape[0] // (words * owners * unroll), body, (zero,) * slots)
        for s in range(slots):
            out_ref[owner, s] = sums[s]


def finish(x_ref, out_ref):
    parts, rows, edge = x_ref.shape
    total = x_ref[: parts // 2] + x_ref[parts // 2 :]
    out_ref[...] = total.reshape(edge, edge).T.astype(out_ref.dtype)


def on_device(lam_tiles, int_tiles, task_list, live_count, tile_mask, owner_map):
    tile_devs = lax.axis_size("tiles")
    reps = lax.axis_size("rep")
    rep_index = lax.axis_index("rep")
    lam_dev, edge, _ = lam_tiles.shape
    int_dev = int_tiles.shape[0]
    res_tile = owner_map.shape[0] // tile_devs
    rows = edge // reps
    words = rows // 2 + 1

    tasks = task_list.T
    chips = tile_devs // 2
    same_core = [[2 * chip + core for chip in range(chips)] for core in range(2)]
    request = pl.pallas_call(
        functools.partial(ask, int_dev=int_dev),
        out_shape=jax.ShapeDtypeStruct((chips, 128), jnp.int32),
        in_specs=[VMEM],
        out_specs=VMEM,
        compiler_params=ROOM,
        name="ask",
    )(tasks)
    request = lax.all_to_all(
        request.reshape(chips, 1, 128), "tiles", split_axis=0, concat_axis=0, tiled=True, axis_index_groups=same_core
    ).reshape(chips, 128)
    code = pl.pallas_call(
        functools.partial(read_tasks, int_dev=int_dev, res_tile=res_tile),
        out_shape=jax.ShapeDtypeStruct((1, tile_devs), jnp.int32),
        in_specs=[SMEM, SMEM, VMEM, VMEM],
        out_specs=VMEM,
        name="read_tasks",
    )(live_count, tile_mask, tasks, owner_map[None, :])
    codes = [code] + [ring(code, k) for k in range(1, reps)]

    lam_all = pl.pallas_call(
        prepare_lambda,
        out_shape=jax.ShapeDtypeStruct((2 * lam_dev + 1, edge, edge), jnp.bfloat16),
        in_specs=[VMEM],
        out_specs=VMEM,
        compiler_params=ROOM,
        name="prepare_lambda",
    )(lam_tiles)
    other = lax.ppermute(int_tiles, "tiles", [(i, i ^ 1) for i in range(tile_devs)])
    columns = pl.pallas_call(
        prepare_integrals,
        out_shape=jax.ShapeDtypeStruct((2, int_dev, rows, edge), jnp.bfloat16),
        in_specs=[SMEM, VMEM, VMEM],
        out_specs=VMEM,
        scratch_shapes=[pltpu.VMEM((int_dev, edge, edge), jnp.bfloat16)],
        compiler_params=ROOM,
        name="prepare_integrals",
    )(jnp.stack([lax.axis_index("tiles") % 2, rep_index * rows]), int_tiles, other)
    picked = pl.pallas_call(
        pick,
        out_shape=jax.ShapeDtypeStruct((chips, 2 * rows, edge), jnp.bfloat16),
        in_specs=[VMEM, VMEM],
        out_specs=VMEM,
        scratch_shapes=[
            pltpu.VMEM((1, 128), jnp.int32),
            pltpu.SMEM((1, 128), jnp.int32),
            pltpu.SemaphoreType.DMA,
        ],
        compiler_params=ROOM,
        name="pick",
    )(request, columns)
    fetched = lax.all_to_all(
        picked, "tiles", split_axis=0, concat_axis=0, tiled=True, axis_index_groups=same_core
    ).reshape(tile_devs, rows, edge)

    totals = pl.pallas_call(
        functools.partial(contract, slots=res_tile),
        out_shape=jax.ShapeDtypeStruct((tile_devs * words, edge), jnp.int32),
        in_specs=[SMEM] * reps + [VMEM, VMEM],
        out_specs=VMEM,
        compiler_params=ROOM,
        name="contract",
    )(*codes, lam_all, fetched)
    totals = totals.reshape(chips, 2 * words, 1, edge)
    partial_tiles = lax.all_to_all(
        totals, "tiles", split_axis=0, concat_axis=0, tiled=True, axis_index_groups=same_core
    ).reshape(tile_devs * words, edge)
    summed = pl.pallas_call(
        add_slots,
        out_shape=jax.ShapeDtypeStruct((2, res_tile, rows, edge), jnp.float32),
        in_specs=[VMEM],
        out_specs=VMEM,
        compiler_params=ROOM,
        name="add_slots",
    )(partial_tiles)
    same_chip = [[2 * reps * chip + i for i in range(2 * reps)] for chip in range(chips)]
    mine = lax.all_to_all(
        summed.reshape(2 * res_tile, rows, edge),
        ("tiles", "rep"),
        split_axis=0,
        concat_axis=0,
        tiled=True,
        axis_index_groups=same_chip,
    )
    mine = pl.pallas_call(
        finish,
        out_shape=jax.ShapeDtypeStruct((edge, edge), jnp.bfloat16),
        in_specs=[VMEM],
        out_specs=VMEM,
        compiler_params=ROOM,
        name="finish",
    )(mine)
    return mine[None]


def solution(mesh):
    placed = (
        P("tiles", None, None),
        P("tiles", None, None),
        P(("tiles", "rep"), None),
        P(("tiles", "rep")),
        P("tiles"),
        P(),
    )
    return jax.shard_map(
        on_device,
        mesh=mesh,
        in_specs=placed,
        out_specs=P(("tiles", "rep"), None, None),
        check_vma=False,
    )
```

```python
import functools

import jax
import jax.numpy as jnp
from jax import lax
from jax.experimental import pallas as pl
from jax.experimental.pallas import tpu as pltpu
from jax.sharding import PartitionSpec as P

VMEM = pl.BlockSpec(memory_space=pltpu.VMEM)
OCTAVE = 64.0
FULL = 32760.0
SMALLEST = 2.0**-110
ROOM = pltpu.CompilerParams(vmem_limit_bytes=8 * 2**20)
SMEM = pl.BlockSpec(memory_space=pltpu.SMEM)


def power(size):
    return size.bit_length() - 1


def ring(values, steps):
    reps = lax.axis_size("rep")
    return lax.ppermute(values, "rep", [(i, (i + steps) % reps) for i in range(reps)])


def prepare_lambda(lam_ref, out_ref):
    count = lam_ref.shape[0]
    for tile in range(count):
        out_ref[tile] = lam_ref[tile].T
        out_ref[count + tile] = lam_ref[tile]
    out_ref[2 * count] = jnp.zeros_like(out_ref[2 * count])


def prepare_integrals(place_ref, own_ref, other_ref, out_ref, turned):
    _, count, rows, _ = out_ref.shape
    core = place_ref[0]
    start = pl.multiple_of(place_ref[1], rows)
    for place, tiles in ((core, own_ref), (1 - core, other_ref)):
        for tile in range(count):
            turned[tile] = tiles[tile].T
            out_ref[place, tile] = turned[tile, pl.ds(start, rows), :]


def ask(task_ref, request_ref, int_dev):
    peers, task_dev = request_ref.shape[0], task_ref.shape[1]
    w_ids = task_ref[1:2, :]
    w_owner = lax.shift_right_logical(w_ids, power(int_dev))
    place = lax.bitwise_and(w_owner, 1) * power(int_dev)
    named = lax.shift_left(lax.bitwise_and(w_ids, int_dev - 1), place)
    peer = lax.broadcasted_iota(jnp.int32, (peers, task_dev), 0)
    wanted = jnp.where(peer == lax.shift_right_logical(w_owner, 1), named, 0)
    wanted = jnp.sum(wanted, axis=1, keepdims=True)
    request_ref[...] = jnp.broadcast_to(wanted, (peers, task_dev))


def read_tasks(live_ref, mask_ref, task_ref, map_ref, code_ref, int_dev, res_tile):
    lam_dev = mask_ref.shape[0]
    task_dev = task_ref.shape[1]
    peers = code_ref.shape[1]
    res_total = map_ref.shape[1]
    placed = map_ref[...]
    parts = jnp.concatenate(
        [placed // res_tile, placed % res_tile, jnp.zeros((6, res_total), jnp.int32)], axis=0
    )
    named = lax.broadcasted_iota(jnp.int32, (res_total, task_dev), 0) == task_ref[2:3, :]
    looked_up = jnp.dot(
        parts.astype(jnp.float32).astype(jnp.bfloat16),
        jnp.where(named, 1.0, 0.0).astype(jnp.bfloat16),
        preferred_element_type=jnp.float32,
    ).astype(jnp.int32)
    o_owner, slot = looked_up[0:1, :], looked_up[1:2, :]
    w_owner = task_ref[1:2, :] // int_dev
    lam_local = task_ref[0:1, :] % lam_dev
    hits_o = lax.broadcasted_iota(jnp.int32, (peers, task_dev), 0) == o_owner
    kept = jnp.zeros((1, task_dev), jnp.int32)
    for tile in range(lam_dev):
        kept = jnp.where(lam_local == tile, mask_ref[tile], kept)
    live = lax.broadcasted_iota(jnp.int32, (1, task_dev), 1) < live_ref[0]
    variant = jnp.where((kept == 1) & live, lam_local + lam_dev * task_ref[3:4, :], 2 * lam_dev)
    rows = jnp.concatenate([variant, w_owner, slot, jnp.zeros((5, task_dev), jnp.int32)], axis=0)
    by_owner = lax.dot_general(
        rows.astype(jnp.float32).astype(jnp.bfloat16),
        jnp.where(hits_o, 1.0, 0.0).astype(jnp.bfloat16),
        (((1,), (1,)), ((), ())),
        preferred_element_type=jnp.float32,
    ).astype(jnp.int32)
    code_ref[...] = (by_owner[0:1, :] * peers + by_owner[1:2, :]) * res_tile + by_owner[2:3, :]


def pick(request_ref, tiles_ref, out_ref, row, asked, sem):
    peers, both, edge = out_ref.shape
    _, int_dev, rows, _ = tiles_ref.shape
    got = request_ref[...]
    diagonal = lax.broadcasted_iota(jnp.int32, got.shape, 0) == lax.broadcasted_iota(jnp.int32, got.shape, 1)
    row[...] = jnp.sum(jnp.where(diagonal, got, 0), axis=0, keepdims=True)
    copy = pltpu.make_async_copy(row, asked, sem)
    copy.start()
    copy.wait()

    def body(step, carry):
        for k in range(16):
            peer = step * 16 + k
            word = asked[0, peer]
            out_ref[peer, :rows] = tiles_ref[0, lax.bitwise_and(word, int_dev - 1)]
            out_ref[peer, rows:] = tiles_ref[1, lax.shift_right_logical(word, power(int_dev))]
        return carry

    lax.fori_loop(0, peers // 16, body, 0)


def contract(*refs, slots):
    *code_refs, lam_ref, w_ref, out_ref = refs
    peers, rows, edge = w_ref.shape
    unroll = 32
    half = rows // 2
    words = rows + 1

    def one(owner):
        codes = [ref[0, owner] for ref in code_refs]
        slot = lax.bitwise_and(codes[0], slots - 1)
        codes = [lax.shift_right_logical(code, power(slots)) for code in codes]
        left = [w_ref[lax.bitwise_and(code, peers - 1)] for code in codes]
        right = [lam_ref[lax.shift_right_logical(code, power(peers))] for code in codes]
        total = jnp.dot(
            jnp.concatenate(left, axis=1),
            jnp.concatenate(right, axis=0),
            preferred_element_type=jnp.float32,
        )
        top = jnp.max(jnp.abs(total), axis=0, keepdims=True)
        scale = jnp.ceil(jnp.log2(jnp.maximum(top, SMALLEST)) * OCTAVE)
        whole = jnp.round(total * (jnp.exp2(scale * (-1.0 / OCTAVE)) * FULL)).astype(jnp.int32)
        return whole[:half] * 65536 + whole[half:], scale.astype(jnp.int32) * slots + slot

    def body(step, carry):
        for place in range(unroll):
            first = pl.multiple_of(step * unroll * words, 8) + place * words
            pairs, last = one((step * unroll + place) * 2)
            out_ref[pl.ds(first, half), :] = pairs
            pairs, other = one((step * unroll + place) * 2 + 1)
            out_ref[pl.ds(first + half, half), :] = pairs
            out_ref[pl.ds(first + rows, 1), :] = last * 65536 + other
        return carry

    lax.fori_loop(0, peers // 2 // unroll, body, 0)


def halves(pairs):
    low = lax.shift_right_arithmetic(lax.shift_left(pairs, 16), 16)
    return lax.shift_right_arithmetic(pairs - low, 16), low


def add_slots(x_ref, out_ref):
    owners, slots, rows, edge = out_ref.shape
    half = rows // 2
    words = rows + 1
    unroll = 16
    zero = jnp.zeros((rows, edge), jnp.float32)
    for owner in range(owners):

        def body(step, sums):
            for k in range(unroll):
                first = pl.multiple_of(step * unroll * words, 8) + k * words
                value = jnp.concatenate(halves(x_ref[pl.ds(first + owner * half, half), :]), axis=0)
                last = halves(x_ref[pl.ds(first + rows, 1), :])[owner]
                slot = lax.bitwise_and(last, slots - 1)
                scale = lax.shift_right_arithmetic(last, power(slots)).astype(jnp.float32)
                scale = jnp.exp2(scale * (1.0 / OCTAVE)) * (1.0 / FULL)
                value = value.astype(jnp.float32) * scale
                mine = [jnp.broadcast_to(slot, (rows, edge)) == s for s in range(slots)]
                sums = tuple(jnp.where(m, total + value, total) for m, total in zip(mine, sums))
            return sums

        sums = lax.fori_loop(0, x_ref.shape[0] // (words * unroll), body, (zero,) * slots)
        for s in range(slots):
            out_ref[owner, s] = sums[s]


def finish(x_ref, out_ref):
    parts, rows, edge = x_ref.shape
    total = x_ref[: parts // 2] + x_ref[parts // 2 :]
    out_ref[...] = total.reshape(edge, edge).T.astype(out_ref.dtype)


def on_device(lam_tiles, int_tiles, task_list, live_count, tile_mask, owner_map):
    tile_devs = lax.axis_size("tiles")
    reps = lax.axis_size("rep")
    rep_index = lax.axis_index("rep")
    lam_dev, edge, _ = lam_tiles.shape
    int_dev = int_tiles.shape[0]
    res_tile = owner_map.shape[0] // tile_devs
    rows = edge // reps
    words = rows + 1

    tasks = task_list.T
    chips = tile_devs // 2
    same_core = [[2 * chip + core for chip in range(chips)] for core in range(2)]
    request = pl.pallas_call(
        functools.partial(ask, int_dev=int_dev),
        out_shape=jax.ShapeDtypeStruct((chips, 128), jnp.int32),
        in_specs=[VMEM],
        out_specs=VMEM,
        compiler_params=ROOM,
        name="ask",
    )(tasks)
    request = lax.all_to_all(
        request.reshape(chips, 1, 128), "tiles", split_axis=0, concat_axis=0, tiled=True, axis_index_groups=same_core
    ).reshape(chips, 128)
    code = pl.pallas_call(
        functools.partial(read_tasks, int_dev=int_dev, res_tile=res_tile),
        out_shape=jax.ShapeDtypeStruct((1, tile_devs), jnp.int32),
        in_specs=[SMEM, SMEM, VMEM, VMEM],
        out_specs=VMEM,
        name="read_tasks",
    )(live_count, tile_mask, tasks, owner_map[None, :])
    codes = [code] + [ring(code, k) for k in range(1, reps)]

    lam_all = pl.pallas_call(
        prepare_lambda,
        out_shape=jax.ShapeDtypeStruct((2 * lam_dev + 1, edge, edge), jnp.bfloat16),
        in_specs=[VMEM],
        out_specs=VMEM,
        compiler_params=ROOM,
        name="prepare_lambda",
    )(lam_tiles)
    other = lax.ppermute(int_tiles, "tiles", [(i, i ^ 1) for i in range(tile_devs)])
    columns = pl.pallas_call(
        prepare_integrals,
        out_shape=jax.ShapeDtypeStruct((2, int_dev, rows, edge), jnp.bfloat16),
        in_specs=[SMEM, VMEM, VMEM],
        out_specs=VMEM,
        scratch_shapes=[pltpu.VMEM((int_dev, edge, edge), jnp.bfloat16)],
        compiler_params=ROOM,
        name="prepare_integrals",
    )(jnp.stack([lax.axis_index("tiles") % 2, rep_index * rows]), int_tiles, other)
    picked = pl.pallas_call(
        pick,
        out_shape=jax.ShapeDtypeStruct((chips, 2 * rows, edge), jnp.bfloat16),
        in_specs=[VMEM, VMEM],
        out_specs=VMEM,
        scratch_shapes=[
            pltpu.VMEM((1, 128), jnp.int32),
            pltpu.SMEM((1, 128), jnp.int32),
            pltpu.SemaphoreType.DMA,
        ],
        compiler_params=ROOM,
        name="pick",
    )(request, columns)
    fetched = lax.all_to_all(
        picked, "tiles", split_axis=0, concat_axis=0, tiled=True, axis_index_groups=same_core
    ).reshape(tile_devs, rows, edge)

    totals = pl.pallas_call(
        functools.partial(contract, slots=res_tile),
        out_shape=jax.ShapeDtypeStruct((chips * words, edge), jnp.int32),
        in_specs=[SMEM] * reps + [VMEM, VMEM],
        out_specs=VMEM,
        compiler_params=ROOM,
        name="contract",
    )(*codes, lam_all, fetched)
    totals = totals.reshape(chips, words, 1, edge)
    partial_tiles = lax.all_to_all(
        totals, "tiles", split_axis=0, concat_axis=0, tiled=True, axis_index_groups=same_core
    ).reshape(chips * words, edge)
    summed = pl.pallas_call(
        add_slots,
        out_shape=jax.ShapeDtypeStruct((2, res_tile, rows, edge), jnp.float32),
        in_specs=[VMEM],
        out_specs=VMEM,
        compiler_params=ROOM,
        name="add_slots",
    )(partial_tiles)
    same_chip = [[2 * reps * chip + i for i in range(2 * reps)] for chip in range(chips)]
    mine = lax.all_to_all(
        summed.reshape(2 * res_tile, rows, edge),
        ("tiles", "rep"),
        split_axis=0,
        concat_axis=0,
        tiled=True,
        axis_index_groups=same_chip,
    )
    mine = pl.pallas_call(
        finish,
        out_shape=jax.ShapeDtypeStruct((edge, edge), jnp.bfloat16),
        in_specs=[VMEM],
        out_specs=VMEM,
        compiler_params=ROOM,
        name="finish",
    )(mine)
    return mine[None]


def solution(mesh):
    placed = (
        P("tiles", None, None),
        P("tiles", None, None),
        P(("tiles", "rep"), None),
        P(("tiles", "rep")),
        P("tiles"),
        P(),
    )
    return jax.shard_map(
        on_device,
        mesh=mesh,
        in_specs=placed,
        out_specs=P(("tiles", "rep"), None, None),
        check_vma=False,
    )
```

```python
import functools

import jax
import jax.numpy as jnp
from jax import lax
from jax.experimental import pallas as pl
from jax.experimental.pallas import tpu as pltpu
from jax.sharding import PartitionSpec as P

VMEM = pl.BlockSpec(memory_space=pltpu.VMEM)
OCTAVE = 64.0
FULL = 32760.0
SMALLEST = 2.0**-110
ROOM = pltpu.CompilerParams(vmem_limit_bytes=8 * 2**20)
SMEM = pl.BlockSpec(memory_space=pltpu.SMEM)


def power(size):
    return size.bit_length() - 1


def ring(values, steps):
    reps = lax.axis_size("rep")
    return lax.ppermute(values, "rep", [(i, (i + steps) % reps) for i in range(reps)])


def prepare_lambda(lam_ref, out_ref):
    count = lam_ref.shape[0]
    for tile in range(count):
        out_ref[tile] = lam_ref[tile].T
        out_ref[count + tile] = lam_ref[tile]
    out_ref[2 * count] = jnp.zeros_like(out_ref[2 * count])


def prepare_integrals(place_ref, own_ref, other_ref, out_ref, turned):
    _, count, rows, _ = out_ref.shape
    core = place_ref[0]
    start = pl.multiple_of(place_ref[1], rows)
    for place, tiles in ((core, own_ref), (1 - core, other_ref)):
        for tile in range(count):
            turned[tile] = tiles[tile].T
            out_ref[place, tile] = turned[tile, pl.ds(start, rows), :]


def ask(task_ref, request_ref, int_dev):
    peers, task_dev = request_ref.shape[0], task_ref.shape[1]
    w_ids = task_ref[1:2, :]
    w_owner = lax.shift_right_logical(w_ids, power(int_dev))
    place = lax.bitwise_and(w_owner, 1) * power(int_dev)
    named = lax.shift_left(lax.bitwise_and(w_ids, int_dev - 1), place)
    peer = lax.broadcasted_iota(jnp.int32, (peers, task_dev), 0)
    wanted = jnp.where(peer == lax.shift_right_logical(w_owner, 1), named, 0)
    wanted = jnp.sum(wanted, axis=1, keepdims=True)
    request_ref[...] = jnp.broadcast_to(wanted, (peers, task_dev))


def read_tasks(live_ref, mask_ref, task_ref, map_ref, code_ref, int_dev, res_tile):
    lam_dev = mask_ref.shape[0]
    task_dev = task_ref.shape[1]
    peers = code_ref.shape[1]
    res_total = map_ref.shape[1]
    placed = map_ref[...]
    parts = jnp.concatenate(
        [placed // res_tile, placed % res_tile, jnp.zeros((6, res_total), jnp.int32)], axis=0
    )
    named = lax.broadcasted_iota(jnp.int32, (res_total, task_dev), 0) == task_ref[2:3, :]
    looked_up = jnp.dot(
        parts.astype(jnp.float32).astype(jnp.bfloat16),
        jnp.where(named, 1.0, 0.0).astype(jnp.bfloat16),
        preferred_element_type=jnp.float32,
    ).astype(jnp.int32)
    o_owner, slot = looked_up[0:1, :], looked_up[1:2, :]
    w_owner = task_ref[1:2, :] // int_dev
    lam_local = task_ref[0:1, :] % lam_dev
    hits_o = lax.broadcasted_iota(jnp.int32, (peers, task_dev), 0) == o_owner
    kept = jnp.zeros((1, task_dev), jnp.int32)
    for tile in range(lam_dev):
        kept = jnp.where(lam_local == tile, mask_ref[tile], kept)
    live = lax.broadcasted_iota(jnp.int32, (1, task_dev), 1) < live_ref[0]
    variant = jnp.where((kept == 1) & live, lam_local + lam_dev * task_ref[3:4, :], 2 * lam_dev)
    rows = jnp.concatenate([variant, w_owner, slot, jnp.zeros((5, task_dev), jnp.int32)], axis=0)
    by_owner = lax.dot_general(
        rows.astype(jnp.float32).astype(jnp.bfloat16),
        jnp.where(hits_o, 1.0, 0.0).astype(jnp.bfloat16),
        (((1,), (1,)), ((), ())),
        preferred_element_type=jnp.float32,
    ).astype(jnp.int32)
    code_ref[...] = (by_owner[0:1, :] * peers + by_owner[1:2, :]) * res_tile + by_owner[2:3, :]


def pick(request_ref, tiles_ref, out_ref, filled, row, asked, sem, sent):
    peers, both, edge = filled.shape
    _, int_dev, rows, _ = tiles_ref.shape
    parts = sent.shape[0]
    share = peers // parts
    got = request_ref[...]
    diagonal = lax.broadcasted_iota(jnp.int32, got.shape, 0) == lax.broadcasted_iota(jnp.int32, got.shape, 1)
    row[...] = jnp.sum(jnp.where(diagonal, got, 0), axis=0, keepdims=True)
    copy = pltpu.make_async_copy(row, asked, sem)
    copy.start()
    copy.wait()
    copies = []
    for part in range(parts):
        for peer in range(part * share, (part + 1) * share):
            word = asked[0, peer]
            filled[peer, :rows] = tiles_ref[0, lax.bitwise_and(word, int_dev - 1)]
            filled[peer, rows:] = tiles_ref[1, lax.shift_right_logical(word, power(int_dev))]
        piece = pl.ds(part * share, share)
        copies.append(pltpu.make_async_copy(filled.at[piece], out_ref.at[piece], sent.at[part]))
        copies[-1].start()
    for copy in copies:
        copy.wait()


def contract(*refs, slots):
    *code_refs, lam_ref, w_ref, out_ref = refs
    peers, rows, edge = w_ref.shape
    unroll = 64
    half = rows // 2
    words = rows + 1

    def one(owner):
        codes = [ref[0, owner] for ref in code_refs]
        slot = lax.bitwise_and(codes[0], slots - 1)
        codes = [lax.shift_right_logical(code, power(slots)) for code in codes]
        left = [w_ref[lax.bitwise_and(code, peers - 1)] for code in codes]
        right = [lam_ref[lax.shift_right_logical(code, power(peers))] for code in codes]
        total = jnp.dot(
            jnp.concatenate(left, axis=1),
            jnp.concatenate(right, axis=0),
            preferred_element_type=jnp.float32,
        )
        top = jnp.max(jnp.abs(total), axis=0, keepdims=True)
        scale = jnp.ceil(jnp.log2(jnp.maximum(top, SMALLEST)) * OCTAVE)
        whole = jnp.round(total * (jnp.exp2(scale * (-1.0 / OCTAVE)) * FULL)).astype(jnp.int32)
        return whole[:half] * 65536 + whole[half:], scale.astype(jnp.int32) * slots + slot

    def body(step, carry):
        for place in range(unroll):
            first = pl.multiple_of(step * unroll * words, 8) + place * words
            pairs, last = one((step * unroll + place) * 2)
            out_ref[pl.ds(first, half), :] = pairs
            pairs, other = one((step * unroll + place) * 2 + 1)
            out_ref[pl.ds(first + half, half), :] = pairs
            out_ref[pl.ds(first + rows, 1), :] = last * 65536 + other
        return carry

    lax.fori_loop(0, peers // 2 // unroll, body, 0)


def halves(pairs):
    low = lax.shift_right_arithmetic(lax.shift_left(pairs, 16), 16)
    return lax.shift_right_arithmetic(pairs - low, 16), low


def add_slots(x_ref, out_ref):
    owners, slots, rows, edge = out_ref.shape
    half = rows // 2
    words = rows + 1
    unroll = 16
    zero = jnp.zeros((rows, edge), jnp.float32)
    for owner in range(owners):

        def body(step, sums):
            for k in range(unroll):
                first = pl.multiple_of(step * unroll * words, 8) + k * words
                value = jnp.concatenate(halves(x_ref[pl.ds(first + owner * half, half), :]), axis=0)
                last = halves(x_ref[pl.ds(first + rows, 1), :])[owner]
                slot = lax.bitwise_and(last, slots - 1)
                scale = lax.shift_right_arithmetic(last, power(slots)).astype(jnp.float32)
                scale = jnp.exp2(scale * (1.0 / OCTAVE)) * (1.0 / FULL)
                value = value.astype(jnp.float32) * scale
                mine = [jnp.broadcast_to(slot, (rows, edge)) == s for s in range(slots)]
                sums = tuple(jnp.where(m, total + value, total) for m, total in zip(mine, sums))
            return sums

        sums = lax.fori_loop(0, x_ref.shape[0] // (words * unroll), body, (zero,) * slots)
        for s in range(slots):
            out_ref[owner, s] = sums[s]


def finish(x_ref, out_ref):
    parts, rows, edge = x_ref.shape
    total = x_ref[: parts // 2] + x_ref[parts // 2 :]
    out_ref[...] = total.reshape(edge, edge).T.astype(out_ref.dtype)


def on_device(lam_tiles, int_tiles, task_list, live_count, tile_mask, owner_map):
    tile_devs = lax.axis_size("tiles")
    reps = lax.axis_size("rep")
    rep_index = lax.axis_index("rep")
    lam_dev, edge, _ = lam_tiles.shape
    int_dev = int_tiles.shape[0]
    res_tile = owner_map.shape[0] // tile_devs
    rows = edge // reps
    words = rows + 1

    tasks = task_list.T
    chips = tile_devs // 2
    same_core = [[2 * chip + core for chip in range(chips)] for core in range(2)]
    request = pl.pallas_call(
        functools.partial(ask, int_dev=int_dev),
        out_shape=jax.ShapeDtypeStruct((chips, 128), jnp.int32),
        in_specs=[VMEM],
        out_specs=VMEM,
        compiler_params=ROOM,
        name="ask",
    )(tasks)
    request = lax.all_to_all(
        request.reshape(chips, 1, 128), "tiles", split_axis=0, concat_axis=0, tiled=True, axis_index_groups=same_core
    ).reshape(chips, 128)
    code = pl.pallas_call(
        functools.partial(read_tasks, int_dev=int_dev, res_tile=res_tile),
        out_shape=jax.ShapeDtypeStruct((1, tile_devs), jnp.int32),
        in_specs=[SMEM, SMEM, VMEM, VMEM],
        out_specs=VMEM,
        compiler_params=ROOM,
        name="read_tasks",
    )(live_count, tile_mask, tasks, owner_map[None, :])
    codes = [code] + [ring(code, k) for k in range(1, reps)]

    lam_all = pl.pallas_call(
        prepare_lambda,
        out_shape=jax.ShapeDtypeStruct((2 * lam_dev + 1, edge, edge), jnp.bfloat16),
        in_specs=[VMEM],
        out_specs=VMEM,
        compiler_params=ROOM,
        name="prepare_lambda",
    )(lam_tiles)
    other = lax.ppermute(int_tiles, "tiles", [(i, i ^ 1) for i in range(tile_devs)])
    columns = pl.pallas_call(
        prepare_integrals,
        out_shape=jax.ShapeDtypeStruct((2, int_dev, rows, edge), jnp.bfloat16),
        in_specs=[SMEM, VMEM, VMEM],
        out_specs=VMEM,
        scratch_shapes=[pltpu.VMEM((int_dev, edge, edge), jnp.bfloat16)],
        compiler_params=ROOM,
        name="prepare_integrals",
    )(jnp.stack([lax.axis_index("tiles") % 2, rep_index * rows]), int_tiles, other)
    picked = pl.pallas_call(
        pick,
        out_shape=jax.ShapeDtypeStruct((chips, 2 * rows, edge), jnp.bfloat16),
        in_specs=[VMEM, VMEM],
        out_specs=pl.BlockSpec(memory_space=pltpu.HBM),
        scratch_shapes=[
            pltpu.VMEM((chips, 2 * rows, edge), jnp.bfloat16),
            pltpu.VMEM((1, 128), jnp.int32),
            pltpu.SMEM((1, 128), jnp.int32),
            pltpu.SemaphoreType.DMA,
            pltpu.SemaphoreType.DMA((4,)),
        ],
        compiler_params=ROOM,
        name="pick",
    )(request, columns)
    fetched = lax.all_to_all(
        picked, "tiles", split_axis=0, concat_axis=0, tiled=True, axis_index_groups=same_core
    ).reshape(tile_devs, rows, edge)

    totals = pl.pallas_call(
        functools.partial(contract, slots=res_tile),
        out_shape=jax.ShapeDtypeStruct((chips * words, edge), jnp.int32),
        in_specs=[SMEM] * reps + [VMEM, VMEM],
        out_specs=VMEM,
        compiler_params=ROOM,
        name="contract",
    )(*codes, lam_all, fetched)
    totals = totals.reshape(chips, words, 1, edge)
    partial_tiles = lax.all_to_all(
        totals, "tiles", split_axis=0, concat_axis=0, tiled=True, axis_index_groups=same_core
    ).reshape(chips * words, edge)
    summed = pl.pallas_call(
        add_slots,
        out_shape=jax.ShapeDtypeStruct((2, res_tile, rows, edge), jnp.float32),
        in_specs=[VMEM],
        out_specs=VMEM,
        compiler_params=ROOM,
        name="add_slots",
    )(partial_tiles)
    same_chip = [[2 * reps * chip + i for i in range(2 * reps)] for chip in range(chips)]
    mine = lax.all_to_all(
        summed.reshape(2 * res_tile, rows, edge),
        ("tiles", "rep"),
        split_axis=0,
        concat_axis=0,
        tiled=True,
        axis_index_groups=same_chip,
    )
    mine = pl.pallas_call(
        finish,
        out_shape=jax.ShapeDtypeStruct((edge, edge), jnp.bfloat16),
        in_specs=[VMEM],
        out_specs=VMEM,
        compiler_params=ROOM,
        name="finish",
    )(mine)
    return mine[None]


def solution(mesh):
    placed = (
        P("tiles", None, None),
        P("tiles", None, None),
        P(("tiles", "rep"), None),
        P(("tiles", "rep")),
        P("tiles"),
        P(),
    )
    return jax.shard_map(
        on_device,
        mesh=mesh,
        in_specs=placed,
        out_specs=P(("tiles", "rep"), None, None),
        check_vma=False,
    )
```

```python
import functools

import jax
import jax.numpy as jnp
from jax import lax
from jax.experimental import pallas as pl
from jax.experimental.pallas import tpu as pltpu
from jax.sharding import PartitionSpec as P

VMEM = pl.BlockSpec(memory_space=pltpu.VMEM)
OCTAVE = 64.0
FULL = 32760.0
SMALLEST = 2.0**-110
ROOM = pltpu.CompilerParams(vmem_limit_bytes=8 * 2**20)
SMEM = pl.BlockSpec(memory_space=pltpu.SMEM)


def power(size):
    return size.bit_length() - 1


def ring(values, steps):
    reps = lax.axis_size("rep")
    return lax.ppermute(values, "rep", [(i, (i + steps) % reps) for i in range(reps)])


def prepare_lambda(lam_ref, out_ref):
    count = lam_ref.shape[0]
    for tile in range(count):
        out_ref[tile] = lam_ref[tile].T
        out_ref[count + tile] = lam_ref[tile]
    out_ref[2 * count] = jnp.zeros_like(out_ref[2 * count])


def prepare_integrals(place_ref, own_ref, other_ref, out_ref, turned):
    _, count, rows, _ = out_ref.shape
    core = place_ref[0]
    start = pl.multiple_of(place_ref[1], rows)
    for place, tiles in ((core, own_ref), (1 - core, other_ref)):
        for tile in range(count):
            turned[tile] = tiles[tile].T
            out_ref[place, tile] = turned[tile, pl.ds(start, rows), :]


def ask(task_ref, request_ref, int_dev):
    peers, task_dev = request_ref.shape[0], task_ref.shape[1]
    w_ids = task_ref[1:2, :]
    w_owner = lax.shift_right_logical(w_ids, power(int_dev))
    place = lax.bitwise_and(w_owner, 1) * power(int_dev)
    named = lax.shift_left(lax.bitwise_and(w_ids, int_dev - 1), place)
    peer = lax.broadcasted_iota(jnp.int32, (peers, task_dev), 0)
    wanted = jnp.where(peer == lax.shift_right_logical(w_owner, 1), named, 0)
    wanted = jnp.sum(wanted, axis=1, keepdims=True)
    request_ref[...] = jnp.broadcast_to(wanted, (peers, task_dev))


def read_tasks(live_ref, mask_ref, task_ref, map_ref, code_ref, int_dev, res_tile):
    lam_dev = mask_ref.shape[0]
    task_dev = task_ref.shape[1]
    peers = code_ref.shape[1]
    res_total = map_ref.shape[1]
    placed = map_ref[...]
    parts = jnp.concatenate(
        [placed // res_tile, placed % res_tile, jnp.zeros((6, res_total), jnp.int32)], axis=0
    )
    named = lax.broadcasted_iota(jnp.int32, (res_total, task_dev), 0) == task_ref[2:3, :]
    looked_up = jnp.dot(
        parts.astype(jnp.float32).astype(jnp.bfloat16),
        jnp.where(named, 1.0, 0.0).astype(jnp.bfloat16),
        preferred_element_type=jnp.float32,
    ).astype(jnp.int32)
    o_owner, slot = looked_up[0:1, :], looked_up[1:2, :]
    w_owner = task_ref[1:2, :] // int_dev
    lam_local = task_ref[0:1, :] % lam_dev
    hits_o = lax.broadcasted_iota(jnp.int32, (peers, task_dev), 0) == o_owner
    kept = jnp.zeros((1, task_dev), jnp.int32)
    for tile in range(lam_dev):
        kept = jnp.where(lam_local == tile, mask_ref[tile], kept)
    live = lax.broadcasted_iota(jnp.int32, (1, task_dev), 1) < live_ref[0]
    variant = jnp.where((kept == 1) & live, lam_local + lam_dev * task_ref[3:4, :], 2 * lam_dev)
    rows = jnp.concatenate([variant, w_owner, slot, jnp.zeros((5, task_dev), jnp.int32)], axis=0)
    by_owner = lax.dot_general(
        rows.astype(jnp.float32).astype(jnp.bfloat16),
        jnp.where(hits_o, 1.0, 0.0).astype(jnp.bfloat16),
        (((1,), (1,)), ((), ())),
        preferred_element_type=jnp.float32,
    ).astype(jnp.int32)
    code_ref[...] = (by_owner[0:1, :] * peers + by_owner[1:2, :]) * res_tile + by_owner[2:3, :]


def pick(request_ref, tiles_ref, out_ref, row, asked, sem):
    peers, both, edge = out_ref.shape
    _, int_dev, rows, _ = tiles_ref.shape
    got = request_ref[...]
    diagonal = lax.broadcasted_iota(jnp.int32, got.shape, 0) == lax.broadcasted_iota(jnp.int32, got.shape, 1)
    row[...] = jnp.sum(jnp.where(diagonal, got, 0), axis=0, keepdims=True)
    copy = pltpu.make_async_copy(row, asked, sem)
    copy.start()
    copy.wait()

    def body(step, carry):
        for k in range(16):
            peer = step * 16 + k
            word = asked[0, peer]
            out_ref[peer, :rows] = tiles_ref[0, lax.bitwise_and(word, int_dev - 1)]
            out_ref[peer, rows:] = tiles_ref[1, lax.shift_right_logical(word, power(int_dev))]
        return carry

    lax.fori_loop(0, peers // 16, body, 0)


def contract(*refs, slots):
    *code_refs, lam_ref, w_ref, out_ref = refs
    peers, rows, edge = w_ref.shape
    unroll = 32
    half = rows // 2
    words = rows + 1

    def one(owner):
        codes = [ref[0, owner] for ref in code_refs]
        slot = lax.bitwise_and(codes[0], slots - 1)
        codes = [lax.shift_right_logical(code, power(slots)) for code in codes]
        left = [w_ref[lax.bitwise_and(code, peers - 1)] for code in codes]
        right = [lam_ref[lax.shift_right_logical(code, power(peers))] for code in codes]
        total = jnp.dot(
            jnp.concatenate(left, axis=1),
            jnp.concatenate(right, axis=0),
            preferred_element_type=jnp.float32,
        )
        top = jnp.max(jnp.abs(total), axis=0, keepdims=True)
        scale = jnp.ceil(jnp.log2(jnp.maximum(top, SMALLEST)) * OCTAVE)
        whole = jnp.round(total * (jnp.exp2(scale * (-1.0 / OCTAVE)) * FULL)).astype(jnp.int32)
        return whole[:half] * 65536 + whole[half:], scale.astype(jnp.int32) * slots + slot

    def body(step, carry):
        for place in range(unroll):
            first = pl.multiple_of(step * unroll * words, 8) + place * words
            pairs, last = one((step * unroll + place) * 2)
            out_ref[pl.ds(first, half), :] = pairs
            pairs, other = one((step * unroll + place) * 2 + 1)
            out_ref[pl.ds(first + half, half), :] = pairs
            out_ref[pl.ds(first + rows, 1), :] = last * 65536 + other
        return carry

    lax.fori_loop(0, peers // 2 // unroll, body, 0)


def halves(pairs):
    low = lax.shift_right_arithmetic(lax.shift_left(pairs, 16), 16)
    return lax.shift_right_arithmetic(pairs - low, 16), low


def add_slots(x_ref, out_ref):
    owners, slots, rows, edge = out_ref.shape
    half = rows // 2
    words = rows + 1
    unroll = 32
    zero = jnp.zeros((rows, edge), jnp.float32)
    for owner in range(owners):

        def body(step, sums):
            for k in range(unroll):
                first = pl.multiple_of(step * unroll * words, 8) + k * words
                value = jnp.concatenate(halves(x_ref[pl.ds(first + owner * half, half), :]), axis=0)
                last = halves(x_ref[pl.ds(first + rows, 1), :])[owner]
                slot = lax.bitwise_and(last, slots - 1)
                scale = lax.shift_right_arithmetic(last, power(slots)).astype(jnp.float32)
                scale = jnp.exp2(scale * (1.0 / OCTAVE)) * (1.0 / FULL)
                value = value.astype(jnp.float32) * scale
                mine = [jnp.broadcast_to(slot, (rows, edge)) == s for s in range(slots)]
                sums = tuple(jnp.where(m, total + value, total) for m, total in zip(mine, sums))
            return sums

        sums = lax.fori_loop(0, x_ref.shape[0] // (words * unroll), body, (zero,) * slots)
        for s in range(slots):
            out_ref[owner, s] = sums[s]


def finish(x_ref, out_ref):
    parts, rows, edge = x_ref.shape
    total = x_ref[: parts // 2] + x_ref[parts // 2 :]
    out_ref[...] = total.reshape(edge, edge).T.astype(out_ref.dtype)


def on_device(lam_tiles, int_tiles, task_list, live_count, tile_mask, owner_map):
    tile_devs = lax.axis_size("tiles")
    reps = lax.axis_size("rep")
    rep_index = lax.axis_index("rep")
    lam_dev, edge, _ = lam_tiles.shape
    int_dev = int_tiles.shape[0]
    res_tile = owner_map.shape[0] // tile_devs
    rows = edge // reps
    words = rows + 1

    tasks = task_list.T
    chips = tile_devs // 2
    same_core = [[2 * chip + core for chip in range(chips)] for core in range(2)]
    request = pl.pallas_call(
        functools.partial(ask, int_dev=int_dev),
        out_shape=jax.ShapeDtypeStruct((chips, 128), jnp.int32),
        in_specs=[VMEM],
        out_specs=VMEM,
        compiler_params=ROOM,
        name="ask",
    )(tasks)
    request = lax.all_to_all(
        request.reshape(chips, 1, 128), "tiles", split_axis=0, concat_axis=0, tiled=True, axis_index_groups=same_core
    ).reshape(chips, 128)
    code = pl.pallas_call(
        functools.partial(read_tasks, int_dev=int_dev, res_tile=res_tile),
        out_shape=jax.ShapeDtypeStruct((1, tile_devs), jnp.int32),
        in_specs=[SMEM, SMEM, VMEM, VMEM],
        out_specs=VMEM,
        compiler_params=ROOM,
        name="read_tasks",
    )(live_count, tile_mask, tasks, owner_map[None, :])
    codes = [code] + [ring(code, k) for k in range(1, reps)]

    lam_all = pl.pallas_call(
        prepare_lambda,
        out_shape=jax.ShapeDtypeStruct((2 * lam_dev + 1, edge, edge), jnp.bfloat16),
        in_specs=[VMEM],
        out_specs=VMEM,
        compiler_params=ROOM,
        name="prepare_lambda",
    )(lam_tiles)
    other = lax.ppermute(int_tiles, "tiles", [(i, i ^ 1) for i in range(tile_devs)])
    columns = pl.pallas_call(
        prepare_integrals,
        out_shape=jax.ShapeDtypeStruct((2, int_dev, rows, edge), jnp.bfloat16),
        in_specs=[SMEM, VMEM, VMEM],
        out_specs=VMEM,
        scratch_shapes=[pltpu.VMEM((int_dev, edge, edge), jnp.bfloat16)],
        compiler_params=ROOM,
        name="prepare_integrals",
    )(jnp.stack([lax.axis_index("tiles") % 2, rep_index * rows]), int_tiles, other)
    picked = pl.pallas_call(
        pick,
        out_shape=jax.ShapeDtypeStruct((chips, 2 * rows, edge), jnp.bfloat16),
        in_specs=[VMEM, VMEM],
        out_specs=VMEM,
        scratch_shapes=[
            pltpu.VMEM((1, 128), jnp.int32),
            pltpu.SMEM((1, 128), jnp.int32),
            pltpu.SemaphoreType.DMA,
        ],
        compiler_params=ROOM,
        name="pick",
    )(request, columns)
    fetched = lax.all_to_all(
        picked, "tiles", split_axis=0, concat_axis=0, tiled=True, axis_index_groups=same_core
    ).reshape(tile_devs, rows, edge)

    totals = pl.pallas_call(
        functools.partial(contract, slots=res_tile),
        out_shape=jax.ShapeDtypeStruct((chips * words, edge), jnp.int32),
        in_specs=[SMEM] * reps + [VMEM, VMEM],
        out_specs=VMEM,
        compiler_params=ROOM,
        name="contract",
    )(*codes, lam_all, fetched)
    totals = totals.reshape(chips, words, 1, edge)
    partial_tiles = lax.all_to_all(
        totals, "tiles", split_axis=0, concat_axis=0, tiled=True, axis_index_groups=same_core
    ).reshape(chips * words, edge)
    summed = pl.pallas_call(
        add_slots,
        out_shape=jax.ShapeDtypeStruct((2, res_tile, rows, edge), jnp.float32),
        in_specs=[VMEM],
        out_specs=VMEM,
        compiler_params=ROOM,
        name="add_slots",
    )(partial_tiles)
    same_chip = [[2 * reps * chip + i for i in range(2 * reps)] for chip in range(chips)]
    mine = lax.all_to_all(
        summed.reshape(2 * res_tile, rows, edge),
        ("tiles", "rep"),
        split_axis=0,
        concat_axis=0,
        tiled=True,
        axis_index_groups=same_chip,
    )
    mine = pl.pallas_call(
        finish,
        out_shape=jax.ShapeDtypeStruct((edge, edge), jnp.bfloat16),
        in_specs=[VMEM],
        out_specs=VMEM,
        compiler_params=ROOM,
        name="finish",
    )(mine)
    return mine[None]


def solution(mesh):
    placed = (
        P("tiles", None, None),
        P("tiles", None, None),
        P(("tiles", "rep"), None),
        P(("tiles", "rep")),
        P("tiles"),
        P(),
    )
    return jax.shard_map(
        on_device,
        mesh=mesh,
        in_specs=placed,
        out_specs=P(("tiles", "rep"), None, None),
        check_vma=False,
    )
```

```python
import functools

import jax
import jax.numpy as jnp
from jax import lax
from jax.experimental import pallas as pl
from jax.experimental.pallas import tpu as pltpu
from jax.sharding import PartitionSpec as P

VMEM = pl.BlockSpec(memory_space=pltpu.VMEM)
OCTAVE = 64.0
FULL = 32760.0
SMALLEST = 2.0**-110
ROOM = pltpu.CompilerParams(vmem_limit_bytes=8 * 2**20)
SMEM = pl.BlockSpec(memory_space=pltpu.SMEM)


def power(size):
    return size.bit_length() - 1


def ring(values, steps):
    reps = lax.axis_size("rep")
    return lax.ppermute(values, "rep", [(i, (i + steps) % reps) for i in range(reps)])


def prepare_lambda(lam_ref, out_ref):
    count = lam_ref.shape[0]
    for tile in range(count):
        out_ref[tile] = lam_ref[tile].T
        out_ref[count + tile] = lam_ref[tile]
    out_ref[2 * count] = jnp.zeros_like(out_ref[2 * count])


def prepare_integrals(place_ref, own_ref, other_ref, out_ref, turned):
    _, count, rows, _ = out_ref.shape
    core = place_ref[0]
    start = pl.multiple_of(place_ref[1], rows)
    for place, tiles in ((core, own_ref), (1 - core, other_ref)):
        for tile in range(count):
            turned[tile] = tiles[tile].T
            out_ref[place, tile] = turned[tile, pl.ds(start, rows), :]


def ask(task_ref, request_ref, int_dev):
    peers, task_dev = request_ref.shape[0], task_ref.shape[1]
    w_ids = task_ref[1:2, :]
    w_owner = lax.shift_right_logical(w_ids, power(int_dev))
    place = lax.bitwise_and(w_owner, 1) * power(int_dev)
    named = lax.shift_left(lax.bitwise_and(w_ids, int_dev - 1), place)
    peer = lax.broadcasted_iota(jnp.int32, (peers, task_dev), 0)
    wanted = jnp.where(peer == lax.shift_right_logical(w_owner, 1), named, 0)
    wanted = jnp.sum(wanted, axis=1, keepdims=True)
    request_ref[...] = jnp.broadcast_to(wanted, (peers, task_dev))


def read_tasks(live_ref, mask_ref, task_ref, map_ref, code_ref, int_dev, res_tile):
    lam_dev = mask_ref.shape[0]
    task_dev = task_ref.shape[1]
    peers = code_ref.shape[1]
    res_total = map_ref.shape[1]
    placed = map_ref[...]
    parts = jnp.concatenate(
        [placed // res_tile, placed % res_tile, jnp.zeros((6, res_total), jnp.int32)], axis=0
    )
    named = lax.broadcasted_iota(jnp.int32, (res_total, task_dev), 0) == task_ref[2:3, :]
    looked_up = jnp.dot(
        parts.astype(jnp.float32).astype(jnp.bfloat16),
        jnp.where(named, 1.0, 0.0).astype(jnp.bfloat16),
        preferred_element_type=jnp.float32,
    ).astype(jnp.int32)
    o_owner, slot = looked_up[0:1, :], looked_up[1:2, :]
    w_owner = task_ref[1:2, :] // int_dev
    lam_local = task_ref[0:1, :] % lam_dev
    hits_o = lax.broadcasted_iota(jnp.int32, (peers, task_dev), 0) == o_owner
    kept = jnp.zeros((1, task_dev), jnp.int32)
    for tile in range(lam_dev):
        kept = jnp.where(lam_local == tile, mask_ref[tile], kept)
    live = lax.broadcasted_iota(jnp.int32, (1, task_dev), 1) < live_ref[0]
    variant = jnp.where((kept == 1) & live, lam_local + lam_dev * task_ref[3:4, :], 2 * lam_dev)
    rows = jnp.concatenate([variant, w_owner, slot, jnp.zeros((5, task_dev), jnp.int32)], axis=0)
    by_owner = lax.dot_general(
        rows.astype(jnp.float32).astype(jnp.bfloat16),
        jnp.where(hits_o, 1.0, 0.0).astype(jnp.bfloat16),
        (((1,), (1,)), ((), ())),
        preferred_element_type=jnp.float32,
    ).astype(jnp.int32)
    code_ref[...] = (by_owner[0:1, :] * peers + by_owner[1:2, :]) * res_tile + by_owner[2:3, :]


def pick(request_ref, tiles_ref, out_ref, row, asked, sem):
    peers, both, edge = out_ref.shape
    _, int_dev, rows, _ = tiles_ref.shape
    got = request_ref[...]
    diagonal = lax.broadcasted_iota(jnp.int32, got.shape, 0) == lax.broadcasted_iota(jnp.int32, got.shape, 1)
    row[...] = jnp.sum(jnp.where(diagonal, got, 0), axis=0, keepdims=True)
    copy = pltpu.make_async_copy(row, asked, sem)
    copy.start()
    copy.wait()

    def body(step, carry):
        for k in range(16):
            peer = step * 16 + k
            word = asked[0, peer]
            out_ref[peer, :rows] = tiles_ref[0, lax.bitwise_and(word, int_dev - 1)]
            out_ref[peer, rows:] = tiles_ref[1, lax.shift_right_logical(word, power(int_dev))]
        return carry

    lax.fori_loop(0, peers // 16, body, 0)


def contract(*refs, slots):
    *code_refs, lam_ref, w_ref, out_ref = refs
    peers, rows, edge = w_ref.shape
    unroll = 32
    half = rows // 2
    words = rows + 1

    def one(owner):
        codes = [ref[0, owner] for ref in code_refs]
        slot = lax.bitwise_and(codes[0], slots - 1)
        codes = [lax.shift_right_logical(code, power(slots)) for code in codes]
        left = [w_ref[lax.bitwise_and(code, peers - 1)] for code in codes]
        right = [lam_ref[lax.shift_right_logical(code, power(peers))] for code in codes]
        total = jnp.dot(
            jnp.concatenate(left, axis=1),
            jnp.concatenate(right, axis=0),
            preferred_element_type=jnp.float32,
        )
        top = jnp.max(jnp.abs(total), axis=0, keepdims=True)
        scale = jnp.ceil(jnp.log2(jnp.maximum(top, SMALLEST)) * OCTAVE)
        whole = jnp.round(total * (jnp.exp2(scale * (-1.0 / OCTAVE)) * FULL)).astype(jnp.int32)
        return whole[:half] * 65536 + whole[half:], scale.astype(jnp.int32) * slots + slot

    def body(step, carry):
        for place in range(unroll):
            first = pl.multiple_of(step * unroll * words, 8) + place * words
            pairs, last = one((step * unroll + place) * 2)
            out_ref[pl.ds(first, half), :] = pairs
            pairs, other = one((step * unroll + place) * 2 + 1)
            out_ref[pl.ds(first + half, half), :] = pairs
            out_ref[pl.ds(first + rows, 1), :] = last * 65536 + other
        return carry

    lax.fori_loop(0, peers // 2 // unroll, body, 0)


def halves(pairs):
    low = lax.shift_right_arithmetic(lax.shift_left(pairs, 16), 16)
    return lax.shift_right_arithmetic(pairs - low, 16), low


def add_slots(x_ref, out_ref):
    owners, slots, rows, edge = out_ref.shape
    half = rows // 2
    words = rows + 1
    unroll = 32
    zero = jnp.zeros((rows, edge), jnp.float32)
    for owner in range(owners):

        def body(step, sums):
            for k in range(unroll):
                first = pl.multiple_of(step * unroll * words, 8) + k * words
                value = jnp.concatenate(halves(x_ref[pl.ds(first + owner * half, half), :]), axis=0)
                last = halves(x_ref[pl.ds(first + rows, 1), :])[owner]
                slot = lax.bitwise_and(last, slots - 1)
                scale = lax.shift_right_arithmetic(last, power(slots)).astype(jnp.float32)
                scale = jnp.exp2(scale * (1.0 / OCTAVE)) * (1.0 / FULL)
                value = value.astype(jnp.float32) * scale
                mine = [jnp.broadcast_to(slot, (rows, edge)) == s for s in range(slots)]
                sums = tuple(jnp.where(m, total + value, total) for m, total in zip(mine, sums))
            return sums

        sums = lax.fori_loop(0, x_ref.shape[0] // (words * unroll), body, (zero,) * slots)
        for s in range(slots):
            out_ref[owner, s] = sums[s]


def finish(x_ref, out_ref):
    parts, rows, edge = x_ref.shape
    total = x_ref[: parts // 2] + x_ref[parts // 2 :]
    out_ref[...] = total.reshape(edge, edge).T.astype(out_ref.dtype)


def on_device(lam_tiles, int_tiles, task_list, live_count, tile_mask, owner_map):
    tile_devs = lax.axis_size("tiles")
    reps = lax.axis_size("rep")
    rep_index = lax.axis_index("rep")
    lam_dev, edge, _ = lam_tiles.shape
    int_dev = int_tiles.shape[0]
    res_tile = owner_map.shape[0] // tile_devs
    rows = edge // reps
    words = rows + 1

    tasks = task_list.T
    chips = tile_devs // 2
    same_core = [[2 * chip + core for chip in range(chips)] for core in range(2)]
    request = pl.pallas_call(
        functools.partial(ask, int_dev=int_dev),
        out_shape=jax.ShapeDtypeStruct((chips, 128), jnp.int32),
        in_specs=[VMEM],
        out_specs=VMEM,
        compiler_params=ROOM,
        name="ask",
    )(tasks)
    request, swapped = lax.optimization_barrier((request, int_tiles))
    request = lax.all_to_all(
        request.reshape(chips, 1, 128), "tiles", split_axis=0, concat_axis=0, tiled=True, axis_index_groups=same_core
    ).reshape(chips, 128)
    code = pl.pallas_call(
        functools.partial(read_tasks, int_dev=int_dev, res_tile=res_tile),
        out_shape=jax.ShapeDtypeStruct((1, tile_devs), jnp.int32),
        in_specs=[SMEM, SMEM, VMEM, VMEM],
        out_specs=VMEM,
        compiler_params=ROOM,
        name="read_tasks",
    )(live_count, tile_mask, tasks, owner_map[None, :])
    codes = [code] + [ring(code, k) for k in range(1, reps)]

    lam_all = pl.pallas_call(
        prepare_lambda,
        out_shape=jax.ShapeDtypeStruct((2 * lam_dev + 1, edge, edge), jnp.bfloat16),
        in_specs=[VMEM],
        out_specs=VMEM,
        compiler_params=ROOM,
        name="prepare_lambda",
    )(lam_tiles)
    other = lax.ppermute(swapped, "tiles", [(i, i ^ 1) for i in range(tile_devs)])
    columns = pl.pallas_call(
        prepare_integrals,
        out_shape=jax.ShapeDtypeStruct((2, int_dev, rows, edge), jnp.bfloat16),
        in_specs=[SMEM, VMEM, VMEM],
        out_specs=VMEM,
        scratch_shapes=[pltpu.VMEM((int_dev, edge, edge), jnp.bfloat16)],
        compiler_params=ROOM,
        name="prepare_integrals",
    )(jnp.stack([lax.axis_index("tiles") % 2, rep_index * rows]), int_tiles, other)
    picked = pl.pallas_call(
        pick,
        out_shape=jax.ShapeDtypeStruct((chips, 2 * rows, edge), jnp.bfloat16),
        in_specs=[VMEM, VMEM],
        out_specs=VMEM,
        scratch_shapes=[
            pltpu.VMEM((1, 128), jnp.int32),
            pltpu.SMEM((1, 128), jnp.int32),
            pltpu.SemaphoreType.DMA,
        ],
        compiler_params=ROOM,
        name="pick",
    )(request, columns)
    fetched = lax.all_to_all(
        picked, "tiles", split_axis=0, concat_axis=0, tiled=True, axis_index_groups=same_core
    ).reshape(tile_devs, rows, edge)

    totals = pl.pallas_call(
        functools.partial(contract, slots=res_tile),
        out_shape=jax.ShapeDtypeStruct((chips * words, edge), jnp.int32),
        in_specs=[SMEM] * reps + [VMEM, VMEM],
        out_specs=VMEM,
        compiler_params=ROOM,
        name="contract",
    )(*codes, lam_all, fetched)
    totals = totals.reshape(chips, words, 1, edge)
    partial_tiles = lax.all_to_all(
        totals, "tiles", split_axis=0, concat_axis=0, tiled=True, axis_index_groups=same_core
    ).reshape(chips * words, edge)
    summed = pl.pallas_call(
        add_slots,
        out_shape=jax.ShapeDtypeStruct((2, res_tile, rows, edge), jnp.float32),
        in_specs=[VMEM],
        out_specs=VMEM,
        compiler_params=ROOM,
        name="add_slots",
    )(partial_tiles)
    same_chip = [[2 * reps * chip + i for i in range(2 * reps)] for chip in range(chips)]
    mine = lax.all_to_all(
        summed.reshape(2 * res_tile, rows, edge),
        ("tiles", "rep"),
        split_axis=0,
        concat_axis=0,
        tiled=True,
        axis_index_groups=same_chip,
    )
    mine = pl.pallas_call(
        finish,
        out_shape=jax.ShapeDtypeStruct((edge, edge), jnp.bfloat16),
        in_specs=[VMEM],
        out_specs=VMEM,
        compiler_params=ROOM,
        name="finish",
    )(mine)
    return mine[None]


def solution(mesh):
    placed = (
        P("tiles", None, None),
        P("tiles", None, None),
        P(("tiles", "rep"), None),
        P(("tiles", "rep")),
        P("tiles"),
        P(),
    )
    return jax.shard_map(
        on_device,
        mesh=mesh,
        in_specs=placed,
        out_specs=P(("tiles", "rep"), None, None),
        check_vma=False,
    )
```

```python
import functools

import jax
import jax.numpy as jnp
from jax import lax
from jax.experimental import pallas as pl
from jax.experimental.pallas import tpu as pltpu
from jax.sharding import PartitionSpec as P

VMEM = pl.BlockSpec(memory_space=pltpu.VMEM)
OCTAVE = 64.0
FULL = 32760.0
SMALLEST = 2.0**-110
ROOM = pltpu.CompilerParams(vmem_limit_bytes=8 * 2**20)
SMEM = pl.BlockSpec(memory_space=pltpu.SMEM)


def power(size):
    return size.bit_length() - 1


def ring(values, steps):
    reps = lax.axis_size("rep")
    return lax.ppermute(values, "rep", [(i, (i + steps) % reps) for i in range(reps)])


def prepare_lambda(lam_ref, out_ref):
    count = lam_ref.shape[0]
    for tile in range(count):
        out_ref[tile] = lam_ref[tile].T
        out_ref[count + tile] = lam_ref[tile]
    out_ref[2 * count] = jnp.zeros_like(out_ref[2 * count])


def prepare_integrals(place_ref, own_ref, other_ref, out_ref, turned):
    _, count, rows, _ = out_ref.shape
    core = place_ref[0]
    start = pl.multiple_of(place_ref[1], rows)
    for place, tiles in ((core, own_ref), (1 - core, other_ref)):
        for tile in range(count):
            turned[tile] = tiles[tile].T
            out_ref[place, tile] = turned[tile, pl.ds(start, rows), :]


def ask(task_ref, request_ref, int_dev):
    peers, task_dev = request_ref.shape[0], task_ref.shape[1]
    w_ids = task_ref[1:2, :]
    w_owner = lax.shift_right_logical(w_ids, power(int_dev))
    place = lax.bitwise_and(w_owner, 1) * power(int_dev)
    named = lax.shift_left(lax.bitwise_and(w_ids, int_dev - 1), place)
    peer = lax.broadcasted_iota(jnp.int32, (peers, task_dev), 0)
    wanted = jnp.where(peer == lax.shift_right_logical(w_owner, 1), named, 0)
    wanted = jnp.sum(wanted, axis=1, keepdims=True)
    request_ref[...] = jnp.broadcast_to(wanted, (peers, task_dev))


def read_tasks(live_ref, mask_ref, task_ref, map_ref, code_ref, int_dev, res_tile):
    lam_dev = mask_ref.shape[0]
    task_dev = task_ref.shape[1]
    peers = code_ref.shape[1]
    res_total = map_ref.shape[1]
    placed = map_ref[...]
    parts = jnp.concatenate(
        [placed // res_tile, placed % res_tile, jnp.zeros((6, res_total), jnp.int32)], axis=0
    )
    named = lax.broadcasted_iota(jnp.int32, (res_total, task_dev), 0) == task_ref[2:3, :]
    looked_up = jnp.dot(
        parts.astype(jnp.float32).astype(jnp.bfloat16),
        jnp.where(named, 1.0, 0.0).astype(jnp.bfloat16),
        preferred_element_type=jnp.float32,
    ).astype(jnp.int32)
    o_owner, slot = looked_up[0:1, :], looked_up[1:2, :]
    w_owner = task_ref[1:2, :] // int_dev
    lam_local = task_ref[0:1, :] % lam_dev
    hits_o = lax.broadcasted_iota(jnp.int32, (peers, task_dev), 0) == o_owner
    kept = jnp.zeros((1, task_dev), jnp.int32)
    for tile in range(lam_dev):
        kept = jnp.where(lam_local == tile, mask_ref[tile], kept)
    live = lax.broadcasted_iota(jnp.int32, (1, task_dev), 1) < live_ref[0]
    variant = jnp.where((kept == 1) & live, lam_local + lam_dev * task_ref[3:4, :], 2 * lam_dev)
    rows = jnp.concatenate([variant, w_owner, slot, jnp.zeros((5, task_dev), jnp.int32)], axis=0)
    by_owner = lax.dot_general(
        rows.astype(jnp.float32).astype(jnp.bfloat16),
        jnp.where(hits_o, 1.0, 0.0).astype(jnp.bfloat16),
        (((1,), (1,)), ((), ())),
        preferred_element_type=jnp.float32,
    ).astype(jnp.int32)
    code_ref[...] = (by_owner[0:1, :] * peers + by_owner[1:2, :]) * res_tile + by_owner[2:3, :]


def pick(request_ref, tiles_ref, out_ref, row, asked, sem):
    peers, both, edge = out_ref.shape
    _, int_dev, rows, _ = tiles_ref.shape
    got = request_ref[...]
    diagonal = lax.broadcasted_iota(jnp.int32, got.shape, 0) == lax.broadcasted_iota(jnp.int32, got.shape, 1)
    row[...] = jnp.sum(jnp.where(diagonal, got, 0), axis=0, keepdims=True)
    copy = pltpu.make_async_copy(row, asked, sem)
    copy.start()
    copy.wait()

    def body(step, carry):
        for k in range(16):
            peer = step * 16 + k
            word = asked[0, peer]
            out_ref[peer, :rows] = tiles_ref[0, lax.bitwise_and(word, int_dev - 1)]
            out_ref[peer, rows:] = tiles_ref[1, lax.shift_right_logical(word, power(int_dev))]
        return carry

    lax.fori_loop(0, peers // 16, body, 0)


def contract(*refs, slots):
    *code_refs, lam_ref, w_ref, out_ref = refs
    peers, rows, edge = w_ref.shape
    unroll = 64
    half = rows // 2
    words = rows + 1

    def one(owner):
        codes = [ref[0, owner] for ref in code_refs]
        slot = lax.bitwise_and(codes[0], slots - 1)
        codes = [lax.shift_right_logical(code, power(slots)) for code in codes]
        left = [w_ref[lax.bitwise_and(code, peers - 1)] for code in codes]
        right = [lam_ref[lax.shift_right_logical(code, power(peers))] for code in codes]
        total = jnp.dot(
            jnp.concatenate(left, axis=1),
            jnp.concatenate(right, axis=0),
            preferred_element_type=jnp.float32,
        )
        top = jnp.max(jnp.abs(total), axis=0, keepdims=True)
        scale = jnp.ceil(jnp.log2(jnp.maximum(top, SMALLEST)) * OCTAVE)
        whole = jnp.round(total * (jnp.exp2(scale * (-1.0 / OCTAVE)) * FULL)).astype(jnp.int32)
        return whole[:half] * 65536 + whole[half:], scale.astype(jnp.int32) * slots + slot

    def body(step, carry):
        for place in range(unroll):
            first = pl.multiple_of(step * unroll * words, 8) + place * words
            pairs, last = one((step * unroll + place) * 2)
            out_ref[pl.ds(first, half), :] = pairs
            pairs, other = one((step * unroll + place) * 2 + 1)
            out_ref[pl.ds(first + half, half), :] = pairs
            out_ref[pl.ds(first + rows, 1), :] = last * 65536 + other
        return carry

    lax.fori_loop(0, peers // 2 // unroll, body, 0)


def halves(pairs):
    low = lax.shift_right_arithmetic(lax.shift_left(pairs, 16), 16)
    return lax.shift_right_arithmetic(pairs - low, 16), low


def add_slots(x_ref, out_ref):
    owners, slots, rows, edge = out_ref.shape
    half = rows // 2
    words = rows + 1
    unroll = 32
    zero = jnp.zeros((rows, edge), jnp.float32)
    for owner in range(owners):

        def body(step, sums):
            for k in range(unroll):
                first = pl.multiple_of(step * unroll * words, 8) + k * words
                value = jnp.concatenate(halves(x_ref[pl.ds(first + owner * half, half), :]), axis=0)
                last = halves(x_ref[pl.ds(first + rows, 1), :])[owner]
                slot = lax.bitwise_and(last, slots - 1)
                scale = lax.shift_right_arithmetic(last, power(slots)).astype(jnp.float32)
                scale = jnp.exp2(scale * (1.0 / OCTAVE)) * (1.0 / FULL)
                value = value.astype(jnp.float32) * scale
                mine = [jnp.broadcast_to(slot, (rows, edge)) == s for s in range(slots)]
                sums = tuple(jnp.where(m, total + value, total) for m, total in zip(mine, sums))
            return sums

        sums = lax.fori_loop(0, x_ref.shape[0] // (words * unroll), body, (zero,) * slots)
        for s in range(slots):
            out_ref[owner, s] = sums[s]


def finish(x_ref, out_ref):
    parts, rows, edge = x_ref.shape
    total = x_ref[: parts // 2] + x_ref[parts // 2 :]
    out_ref[...] = total.reshape(edge, edge).T.astype(out_ref.dtype)


def on_device(lam_tiles, int_tiles, task_list, live_count, tile_mask, owner_map):
    tile_devs = lax.axis_size("tiles")
    reps = lax.axis_size("rep")
    rep_index = lax.axis_index("rep")
    lam_dev, edge, _ = lam_tiles.shape
    int_dev = int_tiles.shape[0]
    res_tile = owner_map.shape[0] // tile_devs
    rows = edge // reps
    words = rows + 1

    tasks = task_list.T
    chips = tile_devs // 2
    same_core = [[2 * chip + core for chip in range(chips)] for core in range(2)]
    request = pl.pallas_call(
        functools.partial(ask, int_dev=int_dev),
        out_shape=jax.ShapeDtypeStruct((chips, 128), jnp.int32),
        in_specs=[VMEM],
        out_specs=VMEM,
        compiler_params=ROOM,
        name="ask",
    )(tasks)
    request = lax.all_to_all(
        request.reshape(chips, 1, 128), "tiles", split_axis=0, concat_axis=0, tiled=True, axis_index_groups=same_core
    ).reshape(chips, 128)
    code = pl.pallas_call(
        functools.partial(read_tasks, int_dev=int_dev, res_tile=res_tile),
        out_shape=jax.ShapeDtypeStruct((1, tile_devs), jnp.int32),
        in_specs=[SMEM, SMEM, VMEM, VMEM],
        out_specs=VMEM,
        compiler_params=ROOM,
        name="read_tasks",
    )(live_count, tile_mask, tasks, owner_map[None, :])
    codes = [code] + [ring(code, k) for k in range(1, reps)]

    lam_all = pl.pallas_call(
        prepare_lambda,
        out_shape=jax.ShapeDtypeStruct((2 * lam_dev + 1, edge, edge), jnp.bfloat16),
        in_specs=[VMEM],
        out_specs=VMEM,
        compiler_params=ROOM,
        name="prepare_lambda",
    )(lam_tiles)
    other = lax.ppermute(int_tiles, "tiles", [(i, i ^ 1) for i in range(tile_devs)])
    columns = pl.pallas_call(
        prepare_integrals,
        out_shape=jax.ShapeDtypeStruct((2, int_dev, rows, edge), jnp.bfloat16),
        in_specs=[SMEM, VMEM, VMEM],
        out_specs=VMEM,
        scratch_shapes=[pltpu.VMEM((int_dev, edge, edge), jnp.bfloat16)],
        compiler_params=ROOM,
        name="prepare_integrals",
    )(jnp.stack([lax.axis_index("tiles") % 2, rep_index * rows]), int_tiles, other)
    picked = pl.pallas_call(
        pick,
        out_shape=jax.ShapeDtypeStruct((chips, 2 * rows, edge), jnp.bfloat16),
        in_specs=[VMEM, VMEM],
        out_specs=VMEM,
        scratch_shapes=[
            pltpu.VMEM((1, 128), jnp.int32),
            pltpu.SMEM((1, 128), jnp.int32),
            pltpu.SemaphoreType.DMA,
        ],
        compiler_params=ROOM,
        name="pick",
    )(request, columns)
    fetched = lax.all_to_all(
        picked, "tiles", split_axis=0, concat_axis=0, tiled=True, axis_index_groups=same_core
    ).reshape(tile_devs, rows, edge)

    totals = pl.pallas_call(
        functools.partial(contract, slots=res_tile),
        out_shape=jax.ShapeDtypeStruct((chips * words, edge), jnp.int32),
        in_specs=[SMEM] * reps + [VMEM, VMEM],
        out_specs=VMEM,
        compiler_params=ROOM,
        name="contract",
    )(*codes, lam_all, fetched)
    totals = totals.reshape(chips, words, 1, edge)
    partial_tiles = lax.all_to_all(
        totals, "tiles", split_axis=0, concat_axis=0, tiled=True, axis_index_groups=same_core
    ).reshape(chips * words, edge)
    summed = pl.pallas_call(
        add_slots,
        out_shape=jax.ShapeDtypeStruct((2, res_tile, rows, edge), jnp.float32),
        in_specs=[VMEM],
        out_specs=VMEM,
        compiler_params=ROOM,
        name="add_slots",
    )(partial_tiles)
    same_chip = [[2 * reps * chip + i for i in range(2 * reps)] for chip in range(chips)]
    mine = lax.all_to_all(
        summed.reshape(2 * res_tile, rows, edge),
        ("tiles", "rep"),
        split_axis=0,
        concat_axis=0,
        tiled=True,
        axis_index_groups=same_chip,
    )
    mine = pl.pallas_call(
        finish,
        out_shape=jax.ShapeDtypeStruct((edge, edge), jnp.bfloat16),
        in_specs=[VMEM],
        out_specs=VMEM,
        compiler_params=ROOM,
        name="finish",
    )(mine)
    return mine[None]


def solution(mesh):
    placed = (
        P("tiles", None, None),
        P("tiles", None, None),
        P(("tiles", "rep"), None),
        P(("tiles", "rep")),
        P("tiles"),
        P(),
    )
    return jax.shard_map(
        on_device,
        mesh=mesh,
        in_specs=placed,
        out_specs=P(("tiles", "rep"), None, None),
        check_vma=False,
    )
```
